512 devices in a mesh: dp: 32 (over y_lo, z), seq: 16 (over y_hi, x, core).
Axes of the slice: x: 4, y: 4 (y_hi: 2, y_lo: 2; y = y_hi * 2 + y_lo), z: 16, core: 2. Of those that a mesh axis runs over, the one named last changes fastest.
Arguments:
- hidden: bfloat16 [64, 1024, 8192], P('dp', 'seq'), may hold values from -6 to 6
- queries: bfloat16 [64, 1024, 4096], P('dp', 'seq'), may hold values from -128 to 128
- keys: bfloat16 [64, 1024, 512], P('dp', 'seq'), may hold values from -8 to 8
- upstream: bfloat16 [64, 1024, 4096], P('dp', 'seq'), may hold values from -6 to 6
- w_value: bfloat16 [8192, 512], P(('dp', 'seq')), may hold values from -0.0625 to 0.0625
- segment_ids: int32 [64, 1024], P('dp', 'seq'), may hold values from 0 to 1, as said below
- response_lengths: int32 [64, 2], P('dp'), may hold values from 1 to 256
- advantages: bfloat16 [64, 2], P('dp'), may hold values from -4 to 4
- move_plan: int32 [32, 2], replicated, may hold values from -1 to 1, as said below
Outputs:
- key_grads: bfloat16 [64, 1024, 512], P('dp', 'seq')
- weight_grads: float32 [8192, 512], P(('dp', 'seq'))
The draws below stay inside these ranges and needn't reach their ends.
Inputs may be any that keep to these rules, and one draw needn't show every extreme that they name: At section b data rank r trades slot move_plan[r, b] with rank r XOR 2^b, which trades its slot move_plan[r XOR 2^b, b]; the two ranks of a pair are both -1 (no trade) or both not. `segment_ids`: in every slot the positions before a cut belong to rollout 0 and the rest to rollout 1; the cut lies between 256 and 768. `response_lengths`: A response never exceeds its rollout.
All inputs are finite; a program needn't handle non-finite values.
Results may differ from the reference program's by a relative error of at most 0.034.
Values may be sent and summed in bfloat16 or wider, within the bound.
A program may use at most 64 MiB of HBM per device.

```python
import jax
import jax.numpy as jnp
from jax import lax

D = 8192
HEADS = 32
KVH = 4
HD = 128
SLOTS = 2
ROLLS = 2
SECTIONS = 2
LEN = 1024
SEQS = 64
RANKS = 32
N_DP = 32
N_SEQ = 16


def draw_queries(key, part):
    key = jax.random.fold_in(key, 11)
    tensor = jnp.clip(jax.random.normal(key, (SEQS, LEN, HEADS * HD), jnp.float32), -6.0, 6.0)
    return tensor.astype(jnp.bfloat16)


def draw_keys(key, part):
    key = jax.random.fold_in(key, 13)
    tensor = jnp.clip(jax.random.normal(key, (SEQS, LEN, KVH * HD), jnp.float32), -6.0, 6.0)
    return tensor.astype(jnp.bfloat16)


def draw_segment_ids(key, part):
    key = jax.random.fold_in(key, 17)
    cut_at = jax.random.randint(key, (SEQS, 1), LEN // 4, 3 * LEN // 4 + 1)
    return (jnp.arange(LEN)[None, :] >= cut_at).astype(jnp.int32)


def draw_move_plan(key, part):
    key = jax.random.fold_in(key, 19)
    key_open, second = jax.random.split(key)
    opening = jax.random.randint(key_open, (RANKS, SECTIONS), -1, SLOTS)
    chosen = jax.random.randint(second, (RANKS, SECTIONS), 0, SLOTS)
    rank_ids = jnp.arange(RANKS)
    columns = []
    for section_idx in range(SECTIONS):
        partner = jnp.bitwise_xor(rank_ids, 1 << section_idx)
        lower_rank = jnp.minimum(rank_ids, partner)
        active = opening[lower_rank, section_idx] >= 0
        columns.append(jnp.where(active, chosen[:, section_idx], -1))
    trading = jnp.stack(columns, 1)
    trading = trading.at[0:2, 0].set(SLOTS - 1)
    trading = trading.at[2:4, 0].set(-1)
    return trading.astype(jnp.int32)


def place_ends(result, key, least, high):
    shape = result.shape
    spot = [jax.random.randint(jax.random.fold_in(key, axis), (), 0, shape[axis]) for axis in range(len(shape))]
    result = result.at[tuple(spot)].set(least)
    longest = shape.index(max(shape))
    spot[longest] = (spot[longest] + 1) % shape[longest]
    return result.at[tuple(spot)].set(high)


def with_spikes(result, key, source, target, blocks, factor):
    def block_of(dim):
        return (jnp.arange(result.shape[dim]) // (result.shape[dim] // blocks)).reshape((-1,) + (1,) * (result.ndim - 1 - dim))

    one_side = jax.random.permutation(key, blocks)[block_of(target)]
    other_side = (block_of(target) + blocks // 2) % blocks
    return jnp.where((block_of(source) == one_side) | (block_of(source) == other_side), factor * result, result)


def level_of(own_key, dims, cuts, low, top_value):
    factor_of = 1.0
    for dim, parts in cuts:
        steps = jax.random.uniform(jax.random.fold_in(jax.random.fold_in(own_key, 6), dim), (parts,), jnp.float32, low / len(cuts), top_value / len(cuts))
        factor_of = factor_of * jnp.repeat(jnp.exp(steps), dims[dim] // parts).reshape((-1,) + (1,) * (len(dims) - 1 - dim))
    return factor_of


def normal_values(stream_key, shape, deviation, limit, shards=(), kind=jnp.bfloat16):
    factor_of = level_of(stream_key, shape, shards, -0.22, 0.18) if shards else 1.0
    values = jax.random.normal(stream_key, shape, jnp.float32) * deviation * factor_of
    return jnp.minimum(jnp.maximum(values, -limit), limit).astype(kind)


def heavy_noise(key, extent, scale, reach, shards, heavy, kind=jnp.bfloat16):
    values = scale * jax.random.normal(key, extent, jnp.float32)
    if shards:
        values = values * level_of(key, extent, shards, -0.22, 0.18)
    return jnp.clip(with_spikes(values, jax.random.fold_in(key, 3), *heavy), -reach, reach).astype(kind)


def setup_inputs(seed: int = 0) -> dict:
    key_list = jax.random.split(jax.random.key(seed), 10)
    return {
        "hidden": heavy_noise(key_list[0], (SEQS, LEN, D), 1.0, 6.0, ((0, 32), (1, 16)), (0, 2, 32, 2.75)),
        "queries": draw_queries(jax.random.fold_in(key_list[9], 71), 0),
        "keys": draw_keys(jax.random.fold_in(key_list[9], 71), 0),
        "upstream": normal_values(key_list[3], (SEQS, LEN, HEADS * HD), 1.0, 6.0, ((0, 32), (1, 16))),
        "w_value": normal_values(key_list[4], (D, KVH * HD), D ** -0.5, 0.0625, ((0, 512),)),
        "segment_ids": draw_segment_ids(jax.random.fold_in(key_list[9], 71), 0),
        "response_lengths": place_ends(jax.random.randint(key_list[6], (SEQS, ROLLS), 1, LEN // 4 + 1), jax.random.fold_in(key_list[6], 1), 1, (LEN // 4 + 1) - 1).astype(jnp.int32),
        "advantages": normal_values(key_list[7], (SEQS, ROLLS), 1.0, 4.0, ((0, 32),)),
        "move_plan": draw_move_plan(jax.random.fold_in(key_list[9], 71), 0),
    }


def barrier_round(tensor):
    lowered = tensor.astype(jnp.bfloat16)
    return lax.optimization_barrier(lowered).astype(jnp.float32)


def slot_weights(segment_row, lengths, advantage_row):
    length = segment_row.shape[0]
    member = segment_row[:, None] == jnp.arange(advantage_row.shape[0], dtype=jnp.int32)[None, :]
    counts = jnp.sum(member.astype(jnp.int32), 0).astype(jnp.int32)
    endings = (jnp.cumsum(counts) - 1).astype(jnp.int32)
    last_pos = jnp.sum(jnp.where(member, endings[None, :], 0), 1).astype(jnp.int32)
    resp_tok = jnp.sum(jnp.where(member, lengths[None, :], 0), 1).astype(jnp.int32)
    adv_tok = jnp.sum(jnp.where(member, advantage_row.astype(jnp.float32)[None, :], jnp.float32(0.0)), 1)
    from_end = last_pos - jnp.arange(length, dtype=jnp.int32)
    return jnp.where(from_end < resp_tok, adv_tok, jnp.float32(0.0))


def project_values(slot_hidden, w_value):
    part_width = D // (N_DP * N_SEQ)
    blocks = slot_hidden.reshape(LEN, N_DP, N_SEQ, part_width).astype(jnp.float32)
    weights = w_value.reshape(N_DP, N_SEQ, part_width, KVH * HD).astype(jnp.float32)
    partials = jnp.einsum("tpse,pseo->sto", blocks, weights, precision=lax.Precision.HIGHEST)
    return jnp.sum(barrier_round(partials), 0).astype(jnp.bfloat16)


def trade_slots(tensor, giving, section_idx):
    shaped = tensor.reshape((N_DP, SLOTS) + tensor.shape[1:])
    rank_ids = jnp.arange(N_DP, dtype=jnp.int32)
    partner = jnp.bitwise_xor(rank_ids, jnp.int32(1 << section_idx))
    chosen = jnp.maximum(giving, 0).astype(jnp.int32)
    incoming = shaped[partner, chosen[partner]]
    landing = (jnp.arange(SLOTS, dtype=jnp.int32)[None, :] == chosen[:, None]) & (giving[:, None] >= 0)
    landing = landing.reshape(landing.shape + (1,) * (tensor.ndim - 1))
    return jnp.where(landing, incoming[:, None], shaped).reshape(tensor.shape)


def collect(terms):
    per_dev = HEADS // N_SEQ
    blocks = barrier_round(jnp.sum(terms.reshape(LEN, HEADS // per_dev, per_dev, HD), 2))
    summed = jnp.sum(blocks.reshape(LEN, KVH, (HEADS // KVH) // per_dev, HD), 2)
    return summed.astype(jnp.bfloat16).reshape(LEN, KVH * HD)


def slot_backward(query_rows, key_rows, value_rows, cot_rows, segment_row):
    inv_root = HD ** -0.5
    per_group = HEADS // KVH
    highest_prec = lax.Precision.HIGHEST
    query_all = query_rows.reshape(LEN, HEADS, HD).astype(jnp.float32)
    key_all = jnp.repeat(key_rows.reshape(LEN, KVH, HD).astype(jnp.float32), per_group, axis=1)
    value_all = jnp.repeat(value_rows.reshape(LEN, KVH, HD).astype(jnp.float32), per_group, axis=1)
    cot_all = cot_rows.reshape(LEN, HEADS, HD).astype(jnp.float32)
    positions = jnp.arange(LEN, dtype=jnp.int32)
    allowed = ((segment_row[:, None] == segment_row[None, :]) & (positions[None, :] <= positions[:, None]))[None]
    scores = jnp.einsum("ihd,jhd->hij", query_all, key_all, precision=highest_prec) * inv_root
    scores = jnp.where(allowed, scores, jnp.float32(-1e30))
    highest = jnp.max(scores, 2, keepdims=True)
    weighted = jnp.where(allowed, jnp.exp(scores - highest), jnp.float32(0.0))
    attn_probs = weighted / jnp.sum(weighted, 2, keepdims=True)
    attn_low = barrier_round(attn_probs)
    grad_probs = jnp.einsum("ihd,jhd->hij", cot_all, value_all, precision=highest_prec)
    grad_scores = attn_probs * (grad_probs - jnp.sum(attn_probs * grad_probs, 2, keepdims=True))
    grad_low = barrier_round(grad_scores)
    value_terms = jnp.einsum("hij,ihd->jhd", attn_low, cot_all, precision=highest_prec)
    key_terms = jnp.einsum("hij,ihd->jhd", grad_low, query_all, precision=highest_prec) * inv_root
    return collect(key_terms), collect(value_terms)


def reference(hidden, queries, keys, upstream, w_value, segment_ids, response_lengths, advantages, move_plan):
    values = lax.map(lambda slot_hidden: project_values(slot_hidden, w_value), hidden)
    moving = [hidden, queries, keys, values, upstream, segment_ids, response_lengths, advantages]
    for section_idx in range(SECTIONS):
        moving = [trade_slots(tensor, move_plan[:, section_idx], section_idx) for tensor in moving]
    hidden, queries, keys, values, upstream, segment_ids, response_lengths, advantages = moving
    weights = jax.vmap(slot_weights)(segment_ids, response_lengths, advantages)
    cotangent = (upstream.astype(jnp.float32) * weights[:, :, None]).astype(jnp.bfloat16)
    key_grads, value_grads = lax.map(lambda items: slot_backward(*items), (queries, keys, values, cotangent, segment_ids))

    def accumulate(running, items):
        slot_hidden, slot_grads = items
        added = lax.dot_general(slot_hidden, slot_grads, (((0,), (0,)), ((), ())), preferred_element_type=jnp.float32)
        return running + added, None

    weight_grads, unused = lax.scan(accumulate, jnp.zeros((D, KVH * HD), jnp.float32), (hidden, value_grads))
    return key_grads, weight_grads
```

```python
import functools

import jax
import jax.numpy as jnp
from jax import lax
from jax.experimental import pallas as pl
from jax.experimental.pallas import tpu as pltpu
from jax.sharding import PartitionSpec as P

KVH = 4
HD = 128
MESH = pl.DeviceIdType.MESH
ANY = pl.BlockSpec(memory_space=pl.ANY)
VMEM = pl.BlockSpec(memory_space=pltpu.VMEM)
SMEM = pl.BlockSpec(memory_space=pltpu.SMEM)


def remote(src, dst, send_sem, recv_sem, rank, place):
    return pltpu.make_async_remote_copy(
        src_ref=src,
        dst_ref=dst,
        send_sem=send_sem,
        recv_sem=recv_sem,
        device_id=(rank, place),
        device_id_type=MESH,
    )


def each(low, high, body):
    def step(m, carry):
        body(m)
        return carry

    lax.fori_loop(low, high, step, 0)


def greet(n_dp, n_seq, rank, place):
    barrier = pltpu.get_barrier_semaphore()

    def along_seq(m):
        pl.semaphore_signal(
            barrier, inc=1, device_id=(rank, lax.rem(place + m, n_seq)), device_id_type=MESH
        )

    def along_dp(m):
        pl.semaphore_signal(
            barrier, inc=1, device_id=(lax.rem(rank + m, n_dp), place), device_id_type=MESH
        )

    each(1, n_seq, along_seq)
    each(1, n_dp, along_dp)
    pl.semaphore_wait(barrier, n_seq + n_dp - 2)


def aligned(index, size):
    return pl.ds(pl.multiple_of(index * size, size), size)


def gather_kernel(
    n_dp, n_seq, hidden, queries, keys, upstream, w_value, segs,
    q_full, u_full, k_full, v_full, seg_full, x_out,
    perm, y, x, wg, part, other, red, rs, v_own,
    q_send, q_recv, u_send, u_recv, k_send, k_recv, s_send, s_recv, x_send, x_recv,
    w_send, w_recv, e_send, e_recv, r_send, r_recv, v_send, v_recv, local,
):
    rank, place = lax.axis_index("dp"), lax.axis_index("seq")
    rows = queries.shape[1]
    wide = queries.shape[2] // n_seq
    copies = n_seq // KVH
    chips = n_seq // 2
    core, chip = lax.rem(place, 2), place // 2
    quarter, group = lax.rem(place, copies), place // copies
    span = rows * n_seq // copies
    depth = w_value.shape[0]

    greet(n_dp, n_seq, rank, place)

    def seg_copy(m):
        peer = lax.rem(place + m, n_seq)
        return remote(segs, seg_full.at[place], s_send.at[m], s_recv.at[m], rank, peer)

    def w_copy(m):
        peer = lax.rem(rank + m, n_dp)
        return remote(w_value, wg.at[aligned(rank, depth)], w_send.at[m], w_recv.at[m], peer, place)

    def k_copy(m):
        peer = lax.rem(place + m, n_seq)
        return remote(
            keys.at[:, :, aligned(peer // copies, HD)], k_full.at[:, aligned(place, rows), :],
            k_send.at[m], k_recv.at[m], rank, peer,
        )

    def q_copy(m):
        peer = lax.rem(place + m, n_seq)
        return remote(
            queries.at[:, :, aligned(peer, wide)], q_full.at[:, aligned(place, rows), :],
            q_send.at[m], q_recv.at[m], rank, peer,
        )

    def u_copy(m):
        peer = lax.rem(place + m, n_seq)
        return remote(
            upstream.at[:, :, aligned(peer, wide)], u_full.at[:, aligned(place, rows), :],
            u_send.at[m], u_recv.at[m], rank, peer,
        )

    def x_copy(m):
        peer = lax.rem(place + m, n_seq)
        return remote(y.at[peer], x.at[:, aligned(place, rows), :], x_send.at[m], x_recv.at[m], rank, peer)

    each(1, n_seq, lambda m: seg_copy(m).start())
    each(1, n_dp, lambda m: w_copy(m).start())
    each(1, n_seq, lambda m: k_copy(m).start())
    each(1, n_seq, lambda m: q_copy(m).start())
    own = [
        pltpu.make_async_copy(segs, seg_full.at[place], local.at[0]),
        pltpu.make_async_copy(w_value, wg.at[aligned(rank, depth)], local.at[1]),
        pltpu.make_async_copy(
            keys.at[:, :, aligned(group, HD)], k_full.at[:, aligned(place, rows), :], local.at[2]
        ),
        pltpu.make_async_copy(
            queries.at[:, :, aligned(place, wide)], q_full.at[:, aligned(place, rows), :], local.at[3]
        ),
        pltpu.make_async_copy(
            upstream.at[:, :, aligned(place, wide)], u_full.at[:, aligned(place, rows), :], local.at[4]
        ),
    ]
    for copy in own:
        copy.start()

    runs = HD // depth
    size = runs * HD
    i = lax.broadcasted_iota(jnp.int32, (size, size), 0)
    j = lax.broadcasted_iota(jnp.int32, (size, size), 1)
    to = ((i // depth) % runs) * HD + (i // HD) * depth + i % depth
    perm[...] = jnp.where(j == to, 1.0, 0.0).astype(jnp.bfloat16)
    halves = n_seq // runs
    blocks = n_dp // runs
    for half in range(halves):
        for slot in range(2):
            stacked = jnp.concatenate(
                [
                    jnp.concatenate(
                        [
                            hidden[slot, :, ((b * runs + a) * halves + half) * HD : ((b * runs + a) * halves + half + 1) * HD]
                            for a in range(runs)
                        ],
                        1,
                    )
                    for b in range(blocks)
                ],
                0,
            )
            sorted_rows = jnp.dot(stacked, perm[...], preferred_element_type=jnp.float32).astype(jnp.bfloat16)
            for b in range(blocks):
                for a in range(runs):
                    y[half * runs + a, slot, :, b * HD : (b + 1) * HD] = sorted_rows[
                        b * rows : (b + 1) * rows, a * HD : (a + 1) * HD
                    ]
    each(1, n_seq, lambda m: x_copy(m).start())
    own_x = pltpu.make_async_copy(y.at[place], x.at[:, aligned(place, rows), :], local.at[5])
    own_x.start()
    own[1].wait()
    own_x.wait()
    each(1, n_dp, lambda m: w_copy(m).wait_recv())
    each(1, n_seq, lambda m: x_copy(m).wait_recv())
    each(1, n_seq, lambda m: u_copy(m).start())
    keep = pltpu.make_async_copy(x, x_out, local.at[6])
    keep.start()

    def project(n):
        slot, which = n // copies, lax.rem(n, copies)
        part[slot, which // 2, lax.rem(which, 2)] = jnp.dot(
            x[slot, aligned(which, span), :], wg[...], preferred_element_type=jnp.float32
        ).astype(jnp.bfloat16)

    each(0, 2 * copies, project)
    exchange = remote(part.at[:, :, 1 - core], other, e_send.at[0], e_recv.at[0], rank, place + 1 - 2 * core)
    exchange.start()
    exchange.wait_recv()

    def pair_sum(n):
        slot, which = n // 2, lax.rem(n, 2)
        red[slot, which] = (
            part[slot, which, core].astype(jnp.float32) + other[slot, which].astype(jnp.float32)
        ).astype(jnp.bfloat16)

    each(0, copies, pair_sum)

    def r_copy(m):
        peer = lax.rem(chip + m, chips)
        return remote(
            red.at[:, lax.rem(peer, 2), :, aligned(peer // 2, HD)], rs.at[m],
            r_send.at[m], r_recv.at[m], rank, 2 * peer + core,
        )

    each(1, chips, lambda m: r_copy(m).start())
    mine = pltpu.make_async_copy(red.at[:, lax.rem(chip, 2), :, aligned(group, HD)], rs.at[0], local.at[7])
    mine.start()
    mine.wait()
    each(1, chips, lambda m: r_copy(m).wait_recv())
    for slot in range(2):
        total = rs[0, slot].astype(jnp.float32)
        for m in range(1, chips):
            total = total + rs[m, slot].astype(jnp.float32)
        v_own[slot] = total.astype(jnp.bfloat16)

    def v_copy(m):
        peer = group * copies + lax.rem(quarter + m, copies)
        return remote(v_own, v_full.at[:, aligned(quarter, span), :], v_send.at[m], v_recv.at[m], rank, peer)

    each(1, copies, lambda m: v_copy(m).start())
    own_v = pltpu.make_async_copy(v_own, v_full.at[:, aligned(quarter, span), :], local.at[8])
    own_v.start()
    each(1, n_seq, lambda m: seg_copy(m).wait())
    each(1, n_seq, lambda m: k_copy(m).wait())
    each(1, n_seq, lambda m: q_copy(m).wait())
    each(1, n_seq, lambda m: u_copy(m).wait())
    each(1, n_dp, lambda m: w_copy(m).wait_send())
    each(1, n_seq, lambda m: x_copy(m).wait_send())
    exchange.wait_send()
    each(1, chips, lambda m: r_copy(m).wait_send())
    each(1, copies, lambda m: v_copy(m).wait())
    own_v.wait()
    keep.wait()
    for n in (0, 2, 3, 4):
        own[n].wait()


def attention_kernel(q_ref, u_ref, k_ref, v_ref, seg_ref, length_ref, adv_ref, dk_ref, dv_ref, dk_sum, dv_sum):
    slot = pl.program_id(0)
    length = q_ref.shape[1]
    tile = 256
    scale = HD ** (-0.5)
    to_exp2 = scale * 1.4426950408889634
    cut = length - jnp.sum(seg_ref[:, slot, :])
    position = lax.broadcasted_iota(jnp.int32, (length, HD), 0)
    second = position >= cut
    last = jnp.where(second, length - 1, cut - 1)
    sampled = jnp.where(second, length_ref[slot, 1], length_ref[slot, 0])
    gain = jnp.where(second, adv_ref[slot, 1], adv_ref[slot, 0])
    weight = jnp.where(last - position < sampled, gain, jnp.float32(0.0))
    keys, values = k_ref[0], v_ref[0]
    over_last = (((1,), (1,)), ((), ()))
    dk_sum[...] = jnp.zeros_like(dk_sum)
    dv_sum[...] = jnp.zeros_like(dv_sum)
    for head in range(q_ref.shape[2] // HD):
        lanes = slice(head * HD, (head + 1) * HD)
        for block in range(length // tile):
            at = slice(block * tile, (block + 1) * tile)
            seen = (block + 1) * tile
            query = q_ref[0, at, lanes]
            cot = (u_ref[0, at, lanes].astype(jnp.float32) * weight[at]).astype(jnp.bfloat16)
            scores = lax.dot_general(keys[:seen], query, over_last, preferred_element_type=jnp.float32)
            j = lax.broadcasted_iota(jnp.int32, (seen, tile), 0)
            i = lax.broadcasted_iota(jnp.int32, (1, tile), 1) + block * tile
            least = jnp.where(i >= cut, cut, 0)
            scores = jnp.where((j >= least) & (j <= i), scores, jnp.float32(-1e30))
            highest = jnp.max(scores, 0, keepdims=True)
            weighted = jnp.exp2((scores - highest) * to_exp2)
            probs = weighted * (1.0 / jnp.sum(weighted, 0, keepdims=True))
            dprobs = lax.dot_general(values[:seen], cot, over_last, preferred_element_type=jnp.float32)
            dscores = probs * (dprobs - jnp.sum(probs * dprobs, 0, keepdims=True))
            dv_sum[:seen] += jnp.dot(probs.astype(jnp.bfloat16), cot, preferred_element_type=jnp.float32)
            dk_sum[:seen] += jnp.dot(dscores.astype(jnp.bfloat16), query, preferred_element_type=jnp.float32)
    dk_ref[0] = (dk_sum[...] * scale).astype(jnp.bfloat16)
    dv_ref[0] = dv_sum[...].astype(jnp.bfloat16)


def reduce_kernel(
    n_dp, n_seq, plan, dk_part, dv_part, x_ref,
    key_out, weight_out,
    dv_got, vg, dk_got, kg, give, got, dw, dw_got,
    g_send, g_recv, k_send, k_recv, a_send, a_recv, f_send, f_recv, t_send, t_recv, w_send, w_recv, local,
):
    rank, place = lax.axis_index("dp"), lax.axis_index("seq")
    length = dk_part.shape[1]
    rows = length // n_seq
    copies = n_seq // KVH
    chips = n_seq // 2
    core, chip = lax.rem(place, 2), place // 2
    quarter, group = lax.rem(place, copies), place // copies
    span = length // copies
    sibling = place + 1 - 2 * core
    depth = dw.shape[1]

    greet(n_dp, n_seq, rank, place)

    def g_copy(m):
        which = lax.rem(quarter + m, copies)
        return remote(
            dv_part.at[:, aligned(which, span), :], dv_got.at[m],
            g_send.at[m], g_recv.at[m], rank, group * copies + which,
        )

    def k_copy(m):
        peer = lax.rem(place + m, n_seq)
        return remote(
            dk_part.at[:, aligned(peer, rows), :], dk_got.at[place], k_send.at[m], k_recv.at[m], rank, peer
        )

    each(1, copies, lambda m: g_copy(m).start())
    each(1, n_seq, lambda m: k_copy(m).start())
    own_dk = pltpu.make_async_copy(dk_part.at[:, aligned(place, rows), :], dk_got.at[place], local.at[0])
    own_dk.start()
    own_dv = pltpu.make_async_copy(dv_part.at[:, aligned(quarter, span), :], dv_got.at[0], local.at[1])
    own_dv.start()
    own_dv.wait()
    each(1, copies, lambda m: g_copy(m).wait_recv())
    for slot in range(2):
        total = dv_got[0, slot].astype(jnp.float32)
        for m in range(1, copies):
            total = total + dv_got[m, slot].astype(jnp.float32)
        vg[place, slot] = total.astype(jnp.bfloat16)

    def a_copy(m):
        peer = lax.rem(chip + m, chips)
        return remote(vg.at[place], vg.at[place], a_send.at[m], a_recv.at[m], rank, 2 * peer + core)

    def f_copy(m):
        origin = 2 * lax.rem(chip - m + chips, chips) + core
        return remote(vg.at[origin], vg.at[origin], f_send.at[m], f_recv.at[m], rank, sibling)

    each(1, chips, lambda m: a_copy(m).start())
    f_copy(0).start()

    own_dk.wait()
    each(1, n_seq, lambda m: k_copy(m).wait_recv())
    for slot in range(2):
        for head in range(KVH):
            total = dk_got[head * copies, slot].astype(jnp.float32)
            for m in range(1, copies):
                total = total + dk_got[head * copies + m, slot].astype(jnp.float32)
            kg[slot, :, head * HD : (head + 1) * HD] = total.astype(jnp.bfloat16)

    def trade(section):
        low = lax.rem(rank // (1 << section), 2)
        partner = rank + (1 << section) * (1 - 2 * low)
        return remote(
            give.at[section], got.at[section], t_send.at[section], t_recv.at[section], partner, place
        )

    def offer(section):
        giving = jnp.full(kg.shape[1:], plan[rank, section], jnp.int32)
        first, second = kg[0].astype(jnp.float32), kg[1].astype(jnp.float32)
        give[section] = jnp.where(giving == 1, second, first).astype(jnp.bfloat16)
        trade(section).start()

    def accept(section):
        trade(section).wait_recv()
        giving = jnp.full(kg.shape[1:], plan[rank, section], jnp.int32)
        for slot in range(2):
            arrived, held = got[section].astype(jnp.float32), kg[slot].astype(jnp.float32)
            kg[slot] = jnp.where(giving == slot, arrived, held).astype(jnp.bfloat16)

    offer(0)

    def forward(m):
        a_copy(m).wait_recv()
        f_copy(m).start()

    each(1, chips, forward)
    accept(0)
    offer(1)
    each(0, chips, lambda m: f_copy(m).wait_recv())

    total = None
    for slot in range(2):
        for which in range(copies):
            grads = jnp.concatenate([vg[head * copies + which, slot] for head in range(KVH)], 1)
            term = lax.dot_general(
                x_ref[slot, which * span : (which + 1) * span, :], grads,
                (((0,), (0,)), ((), ())), preferred_element_type=jnp.float32,
            )
            total = term if total is None else total + term
    dw[...] = total.astype(jnp.bfloat16).reshape(dw.shape)

    def w_copy(m):
        peer = lax.rem(rank + m, n_dp)
        return remote(dw.at[peer], dw_got.at[m], w_send.at[m], w_recv.at[m], peer, place)

    each(1, n_dp, lambda m: w_copy(m).start())
    accept(1)
    key_out[...] = kg[...]
    total = dw[rank].astype(jnp.float32)
    each(1, n_dp, lambda m: w_copy(m).wait_recv())
    total = lax.fori_loop(1, n_dp, lambda m, t: t + dw_got[m].astype(jnp.float32), total)
    weight_out[...] = total

    each(1, copies, lambda m: g_copy(m).wait_send())
    each(1, n_seq, lambda m: k_copy(m).wait_send())
    each(1, chips, lambda m: a_copy(m).wait_send())
    each(0, chips, lambda m: f_copy(m).wait_send())
    each(1, n_dp, lambda m: w_copy(m).wait_send())
    trade(0).wait_send()
    trade(1).wait_send()


def on_device(
    hidden, queries, keys, upstream, w_value, segment_ids, response_lengths, advantages, move_plan
):
    n_dp, n_seq = lax.axis_size("dp"), lax.axis_size("seq")
    slots, rows, features = hidden.shape
    wide = queries.shape[2] // n_seq
    length = rows * n_seq
    copies = n_seq // KVH
    chips = n_seq // 2
    span = length // copies
    depth, columns = w_value.shape
    width = depth * n_dp
    bf16 = jnp.bfloat16
    dma = pltpu.SemaphoreType.DMA
    square = (HD // depth) * HD

    q_full, u_full, k_full, v_full, seg_full, x_full = pl.pallas_call(
        functools.partial(gather_kernel, n_dp, n_seq),
        out_shape=(
            jax.ShapeDtypeStruct((slots, length, wide), bf16),
            jax.ShapeDtypeStruct((slots, length, wide), bf16),
            jax.ShapeDtypeStruct((slots, length, HD), bf16),
            jax.ShapeDtypeStruct((slots, length, HD), bf16),
            jax.ShapeDtypeStruct((n_seq, slots, rows), jnp.int32),
            jax.ShapeDtypeStruct((slots, length, width), bf16),
        ),
        in_specs=[VMEM, ANY, ANY, ANY, VMEM, VMEM],
        out_specs=[ANY] * 6,
        scratch_shapes=[
            pltpu.VMEM((square, square), bf16),
            pltpu.VMEM((n_seq, slots, rows, width), bf16),
            pltpu.VMEM((slots, length, width), bf16),
            pltpu.VMEM((width, columns), bf16),
            pltpu.VMEM((slots, copies // 2, 2, span, columns), bf16),
            pltpu.VMEM((slots, copies // 2, span, columns), bf16),
            pltpu.VMEM((slots, copies // 2, span, columns), bf16),
            pltpu.VMEM((chips, slots, span, HD), bf16),
            pltpu.VMEM((slots, span, HD), bf16),
        ]
        + [dma((n_seq,))] * 10
        + [dma((n_dp,))] * 2
        + [dma((1,))] * 2
        + [dma((chips,))] * 2
        + [dma((copies,))] * 2
        + [dma((9,))],
        compiler_params=pltpu.CompilerParams(
            collective_id=0, has_side_effects=True, vmem_limit_bytes=40 << 20
        ),
        name="gather",
    )(hidden, queries, keys, upstream, w_value, segment_ids)

    block = lambda w: pl.BlockSpec((1, length, w), lambda slot: (slot, 0, 0))
    dk_part, dv_part = pl.pallas_call(
        attention_kernel,
        grid=(slots,),
        out_shape=(
            jax.ShapeDtypeStruct((slots, length, HD), bf16),
            jax.ShapeDtypeStruct((slots, length, HD), bf16),
        ),
        in_specs=[
            block(wide), block(wide), block(HD), block(HD),
            pl.BlockSpec((n_seq, slots, rows), lambda slot: (0, 0, 0)), SMEM, SMEM,
        ],
        out_specs=[block(HD), block(HD)],
        scratch_shapes=[pltpu.VMEM((length, HD), jnp.float32), pltpu.VMEM((length, HD), jnp.float32)],
        compiler_params=pltpu.CompilerParams(vmem_limit_bytes=40 << 20),
        name="attention",
    )(q_full, u_full, k_full, v_full, seg_full, response_lengths, advantages.astype(jnp.float32))

    return pl.pallas_call(
        functools.partial(reduce_kernel, n_dp, n_seq),
        out_shape=(
            jax.ShapeDtypeStruct((slots, rows, columns), bf16),
            jax.ShapeDtypeStruct((depth, columns), jnp.float32),
        ),
        in_specs=[SMEM, VMEM, VMEM, VMEM],
        out_specs=[VMEM, VMEM],
        scratch_shapes=[
            pltpu.VMEM((copies, slots, span, HD), bf16),
            pltpu.VMEM((n_seq, slots, span, HD), bf16),
            pltpu.VMEM((n_seq, slots, rows, HD), bf16),
            pltpu.VMEM((slots, rows, columns), bf16),
            pltpu.VMEM((2, rows, columns), bf16),
            pltpu.VMEM((2, rows, columns), bf16),
            pltpu.VMEM((n_dp, depth, columns), bf16),
            pltpu.VMEM((n_dp, depth, columns), bf16),
        ]
        + [dma((copies,))] * 2
        + [dma((n_seq,))] * 2
        + [dma((chips,))] * 4
        + [dma((2,))] * 2
        + [dma((n_dp,))] * 2
        + [dma((2,))],
        compiler_params=pltpu.CompilerParams(
            collective_id=1, has_side_effects=True, vmem_limit_bytes=40 << 20
        ),
        name="reduce",
    )(move_plan, dk_part, dv_part, x_full)


def solution(mesh):
    placed = (
        P("dp", "seq", None),
        P("dp", "seq", None),
        P("dp", "seq", None),
        P("dp", "seq", None),
        P(("dp", "seq"), None),
        P("dp", "seq"),
        P("dp", None),
        P("dp", None),
        P(),
    )
    return jax.shard_map(
        on_device,
        mesh=mesh,
        in_specs=placed,
        out_specs=(P("dp", "seq", None), P(("dp", "seq"), None)),
        check_vma=False,
    )
```

```python
import functools

import jax
import jax.numpy as jnp
from jax import lax
from jax.experimental import pallas as pl
from jax.experimental.pallas import tpu as pltpu
from jax.sharding import PartitionSpec as P

KVH = 4
HD = 128
TILE = 256
MESH = pl.DeviceIdType.MESH
ANY = pl.BlockSpec(memory_space=pl.ANY)
VMEM = pl.BlockSpec(memory_space=pltpu.VMEM)
SMEM = pl.BlockSpec(memory_space=pltpu.SMEM)
OVER_LAST = (((1,), (1,)), ((), ()))
OVER_FIRST = (((0,), (0,)), ((), ()))


def remote(src, dst, send_sem, recv_sem, rank, place):
    return pltpu.make_async_remote_copy(
        src_ref=src,
        dst_ref=dst,
        send_sem=send_sem,
        recv_sem=recv_sem,
        device_id=(rank, place),
        device_id_type=MESH,
    )


def each(low, high, body):
    def step(m, carry):
        body(m)
        return carry

    lax.fori_loop(low, high, step, 0)


class Copies:
    def __init__(self):
        self.groups = {}
        self.landed = set()

    def add(self, name, low, high, make):
        self.groups[name] = (low, high, make)

    def start(self, name, low, high, make):
        self.add(name, low, high, make)
        each(low, high, lambda m: make(m).start())

    def arrive(self, name):
        low, high, make = self.groups[name]
        self.landed.add(name)
        each(low, high, lambda m: make(m).wait_recv())

    def finish(self):
        for name in self.groups:
            if name not in self.landed:
                self.arrive(name)
        for low, high, make in self.groups.values():
            each(low, high, lambda m: make(m).wait_send())


def greet(n_dp, n_seq, rank, place):
    barrier = pltpu.get_barrier_semaphore()

    def along_seq(m):
        pl.semaphore_signal(
            barrier, inc=1, device_id=(rank, lax.rem(place + m, n_seq)), device_id_type=MESH
        )

    def along_dp(m):
        pl.semaphore_signal(
            barrier, inc=1, device_id=(lax.rem(rank + m, n_dp), place), device_id_type=MESH
        )

    each(1, n_seq, along_seq)
    each(1, n_dp, along_dp)
    pl.semaphore_wait(barrier, n_seq + n_dp - 2)


def aligned(index, size):
    return pl.ds(pl.multiple_of(index * size, size), size)


def kernel(
    n_dp, n_seq, hidden, queries, keys, upstream, w_value, segs, lengths, gains, plan,
    key_out, weight_out,
    rows_in, perm, y, x, wg, seg, q, u, k, v, probs,
    part, other, red, rs, dv_sum, dv_give, dv_got, vg, dk_sum, dk_give, dk_got, dk_own,
    kg, give, got, dw_far, dw_came, dw_near, dw_own, dw_got,
    s_send, s_recv, k_send, k_recv, q_send, q_recv, u_send, u_recv, x_send, x_recv,
    w_send, w_recv, e_send, e_recv, r_send, r_recv, a_send, a_recv, f_send, f_recv,
    o_send, o_recv, t_send, t_recv, y_send, y_recv, z_send, z_recv,
    c_send, c_recv, local,
):
    rank, place = lax.axis_index("dp"), lax.axis_index("seq")
    rows = queries.shape[1]
    length = rows * n_seq
    half = length // 2
    wide = q.shape[1]
    per_core = wide // HD
    chips = n_seq // 2
    core, chip = lax.rem(place, 2), place // 2
    sibling = place + 1 - 2 * core
    slot, head = chip // KVH, lax.rem(chip, KVH)
    depth = w_value.shape[0]
    n_z = n_dp // 2
    lane, side = lax.rem(rank, n_z), rank // n_z
    f32, bf16 = jnp.float32, jnp.bfloat16
    scale = HD ** (-0.5)

    copies = Copies()
    load = pltpu.make_async_copy(hidden, rows_in, local.at[0])
    load.start()
    greet(n_dp, n_seq, rank, place)

    def s_copy(m):
        peer = lax.rem(place + m, n_seq)
        return remote(segs, seg.at[place], s_send.at[m], s_recv.at[m], rank, peer)

    def k_part(peer):
        return keys.at[peer // (2 * KVH), :, aligned(lax.rem(peer // 2, KVH), HD)]

    def k_copy(m):
        peer = lax.rem(place + m, n_seq)
        return remote(k_part(peer), k.at[aligned(place, rows)], k_send.at[m], k_recv.at[m], rank, peer)

    def head_part(array, peer):
        return array.at[peer // (2 * KVH), :, aligned(lax.rem(peer, 2 * KVH), wide)]

    def q_copy(m):
        peer = lax.rem(place + m, n_seq)
        return remote(head_part(queries, peer), q.at[aligned(place, rows)], q_send.at[m], q_recv.at[m], rank, peer)

    def u_copy(m):
        peer = lax.rem(place + m, n_seq)
        return remote(head_part(upstream, peer), u.at[aligned(place, rows)], u_send.at[m], u_recv.at[m], rank, peer)

    def w_copy(m):
        peer = lax.rem(rank + m, n_dp)
        return remote(w_value, wg.at[aligned(rank, depth)], w_send.at[m], w_recv.at[m], peer, place)

    def x_copy(m):
        peer = lax.rem(place + m, n_seq)
        return remote(y.at[peer], x.at[:, aligned(place, rows), :], x_send.at[m], x_recv.at[m], rank, peer)

    copies.start("s", 1, n_seq, s_copy)
    copies.start("k", 1, n_seq, k_copy)
    copies.start("q", 1, n_seq, q_copy)
    copies.start("u", 1, n_seq, u_copy)
    copies.start("w", 1, n_dp, w_copy)
    own = [
        pltpu.make_async_copy(segs, seg.at[place], local.at[1]),
        pltpu.make_async_copy(k_part(place), k.at[aligned(place, rows)], local.at[2]),
        pltpu.make_async_copy(head_part(queries, place), q.at[aligned(place, rows)], local.at[3]),
        pltpu.make_async_copy(head_part(upstream, place), u.at[aligned(place, rows)], local.at[4]),
        pltpu.make_async_copy(w_value, wg.at[aligned(rank, depth)], local.at[5]),
    ]
    for copy in own:
        copy.start()

    runs = HD // depth
    size = runs * HD
    i = lax.broadcasted_iota(jnp.int32, (size, size), 0)
    j = lax.broadcasted_iota(jnp.int32, (size, size), 1)
    to = ((i // depth) % runs) * HD + (i // HD) * depth + i % depth
    perm[...] = jnp.where(j == to, 1.0, 0.0).astype(bf16)
    halves = n_seq // runs
    blocks = n_dp // runs
    load.wait()
    for part_of in range(halves):
        for n in range(2):
            stacked = jnp.concatenate(
                [
                    jnp.concatenate(
                        [rows_in[n, :, t * HD : (t + 1) * HD] for t in range(b * runs * halves + part_of, (b + 1) * runs * halves, halves)],
                        1,
                    )
                    for b in range(blocks)
                ],
                0,
            )
            regrouped = jnp.dot(stacked, perm[...], preferred_element_type=f32).astype(bf16)
            for b in range(blocks):
                for a in range(runs):
                    y[part_of * runs + a, n, :, b * HD : (b + 1) * HD] = regrouped[
                        b * rows : (b + 1) * rows, a * HD : (a + 1) * HD
                    ]

    for copy in own:
        copy.wait()
    own_x = pltpu.make_async_copy(y.at[place], x.at[:, aligned(place, rows), :], local.at[6])
    own_x.start()
    copies.arrive("s")
    copies.arrive("k")
    copies.arrive("q")
    copies.start("x", 1, n_seq, x_copy)
    cut = length - jnp.where(slot == 0, jnp.sum(seg[:, 0, :]), jnp.sum(seg[:, 1, :]))

    def parts_of(block):
        return block * TILE, (block + 1) * TILE, TILE * block * (block + 1) // 2

    def probs_of(h):
        lanes = aligned(h, HD)
        for block in range(length // TILE):
            at, seen, offset = parts_of(block)
            scores = lax.dot_general(k[:seen], q[at:seen, lanes], OVER_LAST, preferred_element_type=f32)
            j = lax.broadcasted_iota(jnp.int32, (seen, TILE), 0)
            i = lax.broadcasted_iota(jnp.int32, (1, TILE), 1) + at
            least = jnp.where(i >= cut, cut, 0)
            scores = jnp.where((j >= least) & (j <= i), scores, f32(-1e30))
            highest = jnp.max(scores, 0, keepdims=True)
            weighted = jnp.exp2((scores - highest) * (scale * 1.4426950408889634))
            probs[h, offset : offset + seen] = weighted * (1.0 / jnp.sum(weighted, 0, keepdims=True))

    each(0, per_core, probs_of)

    copies.arrive("u")
    position = lax.broadcasted_iota(jnp.int32, (length, HD), 0)
    second = position >= cut
    last = jnp.where(second, length - 1, cut - 1)
    sampled = jnp.where(second, lengths[slot, 1], lengths[slot, 0])
    gain = jnp.where(second, gains[slot, 1], gains[slot, 0])
    weight = jnp.where(last - position < sampled, gain, f32(0.0))
    for h in range(per_core):
        lanes = slice(h * HD, (h + 1) * HD)
        u[:, lanes] = (u[:, lanes].astype(f32) * weight).astype(bf16)
    dv_sum[...] = jnp.zeros_like(dv_sum)

    def value_grads(h):
        lanes = aligned(h, HD)
        for block in range(length // TILE):
            at, seen, offset = parts_of(block)
            dv_sum[:seen] += jnp.dot(
                probs[h, offset : offset + seen].astype(bf16), u[at:seen, lanes], preferred_element_type=f32
            )

    each(0, per_core, value_grads)

    dv_give[...] = dv_sum[aligned(1 - core, half)].astype(bf16)
    dv_swap = remote(dv_give, dv_got, c_send.at[0], c_recv.at[0], rank, sibling)
    copies.start("dv_swap", 0, 1, lambda m: dv_swap)
    copies.arrive("dv_swap")
    vg[place] = (dv_sum[aligned(core, half)] + dv_got[...].astype(f32)).astype(bf16)

    def a_copy(m):
        peer = lax.rem(chip + m, chips)
        return remote(vg.at[place], vg.at[place], a_send.at[m], a_recv.at[m], rank, 2 * peer + core)

    def f_copy(m):
        origin = 2 * lax.rem(chip - m + chips, chips) + core
        return remote(vg.at[origin], vg.at[origin], f_send.at[m], f_recv.at[m], rank, sibling)

    copies.start("a", 1, chips, a_copy)
    f_copy(0).start()
    copies.add("f", 0, chips, f_copy)

    own_x.wait()
    copies.arrive("w")
    copies.arrive("x")

    def project(n, which):
        part[n, which] = jnp.dot(x[n, aligned(which, half), :], wg[...], preferred_element_type=f32).astype(bf16)

    def e_copy(n):
        return remote(part.at[n, 1 - core], other.at[n], e_send.at[n], e_recv.at[n], rank, sibling)

    def project_far(n):
        project(n, 1 - core)
        e_copy(n).start()

    each(0, 2, project_far)
    copies.add("e", 0, 2, e_copy)
    each(0, 2, lambda n: project(n, core))

    def forward(m):
        a_copy(m).wait_recv()
        f_copy(m).start()

    each(1, chips, forward)
    copies.landed.add("a")

    def pair_sum(n):
        e_copy(n).wait_recv()
        red[n] = (part[n, core].astype(f32) + other[n].astype(f32)).astype(bf16)

    each(0, 2, pair_sum)
    copies.landed.add("e")

    def r_copy(m):
        peer = lax.rem(chip + m, chips)
        return remote(
            red.at[peer // KVH, :, aligned(lax.rem(peer, KVH), HD)], rs.at[m],
            r_send.at[m], r_recv.at[m], rank, 2 * peer + core,
        )

    copies.start("r", 1, chips, r_copy)
    own_r = pltpu.make_async_copy(red.at[slot, :, aligned(head, HD)], rs.at[0], local.at[7])
    own_r.start()

    copies.arrive("f")

    def weight_terms(column, count):
        total = None
        for n in range(2):
            for which in range(2):
                grads = jnp.concatenate([vg[(n * KVH + g) * 2 + which] for g in range(KVH)], 1)
                term = lax.dot_general(
                    x[n, which * half : (which + 1) * half, pl.ds(pl.multiple_of(column, HD), count)], grads,
                    OVER_FIRST, preferred_element_type=f32,
                )
                total = term if total is None else total + term
        return total

    share = n_z * depth
    pieces = share // HD

    def y_copy(n):
        return remote(
            dw_far.at[n], dw_came.at[n], y_send.at[n], y_recv.at[n], lane + n_z * (1 - side), place
        )

    def far_terms(n):
        dw_far[n] = weight_terms((1 - side) * share + n * HD, HD).astype(bf16)
        y_copy(n).start()

    def near_terms(n):
        dw_near[n] = weight_terms(side * share + n * HD, HD)

    each(0, pieces, far_terms)
    copies.add("y", 0, pieces, y_copy)
    each(0, pieces, near_terms)

    def z_copy(m):
        to_lane = lax.rem(lane + m, n_z)
        return remote(dw_own.at[to_lane], dw_got.at[m], z_send.at[m], z_recv.at[m], to_lane + n_z * side, place)

    def merge(n):
        y_copy(n).wait_recv()
        summed = (dw_near[n] + dw_came[n].astype(f32)).astype(bf16)
        dw_own[pl.ds(n * runs, runs)] = summed.reshape(runs, depth, summed.shape[1])

    each(0, pieces, merge)
    copies.landed.add("y")
    copies.start("z", 1, n_z, z_copy)

    own_r.wait()
    copies.arrive("r")
    total = rs[0].astype(f32)
    for m in range(1, chips):
        total = total + rs[m].astype(f32)
    v[aligned(core, half)] = total.astype(bf16)
    v_swap = remote(
        v.at[aligned(core, half)], v.at[aligned(core, half)], c_send.at[1], c_recv.at[1], rank, sibling
    )
    copies.start("v_swap", 0, 1, lambda m: v_swap)
    dk_sum[...] = jnp.zeros_like(dk_sum)
    copies.arrive("v_swap")

    def key_grads(h):
        lanes = aligned(h, HD)
        for block in range(length // TILE):
            at, seen, offset = parts_of(block)
            p = probs[h, offset : offset + seen]
            dprobs = lax.dot_general(v[:seen], u[at:seen, lanes], OVER_LAST, preferred_element_type=f32)
            dscores = p * (dprobs - jnp.sum(p * dprobs, 0, keepdims=True))
            dk_sum[:seen] += jnp.dot(dscores.astype(bf16), q[at:seen, lanes], preferred_element_type=f32)

    each(0, per_core, key_grads)
    dk_give[...] = (dk_sum[aligned(1 - core, half)] * scale).astype(bf16)
    dk_swap = remote(dk_give, dk_got, c_send.at[2], c_recv.at[2], rank, sibling)
    copies.start("dk_swap", 0, 1, lambda m: dk_swap)
    copies.arrive("dk_swap")
    dk_own[...] = (dk_sum[aligned(core, half)] * scale + dk_got[...].astype(f32)).astype(bf16).reshape(dk_own.shape)

    def o_copy(t):
        return remote(
            dk_own.at[t], kg.at[slot, :, aligned(head, HD)], o_send.at[t], o_recv.at[chip],
            rank, core * chips + t,
        )

    def o_start(t):
        @pl.when(core * chips + t != place)
        def _():
            o_copy(t).start()

        @pl.when(core * chips + t == place)
        def _():
            copy = pltpu.make_async_copy(dk_own.at[t], kg.at[slot, :, aligned(head, HD)], local.at[8])
            copy.start()
            copy.wait()

    each(0, chips, o_start)

    def o_wait_recv(c):
        @pl.when(2 * c + place // chips != place)
        def _():
            remote(
                dk_own.at[0], kg.at[c // KVH, :, aligned(lax.rem(c, KVH), HD)], o_send.at[0], o_recv.at[c],
                rank, 2 * c + place // chips,
            ).wait_recv()

    each(0, chips, o_wait_recv)

    def trade(section):
        low = lax.rem(rank // (1 << section), 2)
        partner = rank + (1 << section) * (1 - 2 * low)
        return remote(
            give.at[section], got.at[section], t_send.at[section], t_recv.at[section], partner, place
        )

    for section in range(2):
        giving = jnp.full(kg.shape[1:], plan[section, rank], jnp.int32)
        first, other_slot = kg[0].astype(f32), kg[1].astype(f32)
        give[section] = jnp.where(giving == 1, other_slot, first).astype(bf16)
        copies.start(("t", section), section, section + 1, trade)
        copies.arrive(("t", section))
        arrived = got[section].astype(f32)
        kg[0] = jnp.where(giving == 0, arrived, first).astype(bf16)
        kg[1] = jnp.where(giving == 1, arrived, other_slot).astype(bf16)
    key_out[...] = kg[...]

    copies.arrive("z")
    total = dw_own[lane].astype(f32)
    for m in range(1, n_z):
        total = total + dw_got[m].astype(f32)
    weight_out[...] = total

    def o_wait_send(t):
        @pl.when(core * chips + t != place)
        def _():
            o_copy(t).wait_send()

    each(0, chips, o_wait_send)
    copies.finish()


def on_device(
    hidden, queries, keys, upstream, w_value, segment_ids, response_lengths, advantages, move_plan
):
    n_dp, n_seq = lax.axis_size("dp"), lax.axis_size("seq")
    slots, rows, features = hidden.shape
    length = rows * n_seq
    half = length // 2
    chips = n_seq // 2
    wide = queries.shape[2] * slots // n_seq
    heads = wide // HD
    depth, columns = w_value.shape
    width = depth * n_dp
    share = width // 2
    bf16, f32 = jnp.bfloat16, jnp.float32
    square = (HD // depth) * HD
    tiles = length // TILE
    triangle = TILE * tiles * (tiles + 1) // 2
    dma = pltpu.SemaphoreType.DMA
    return pl.pallas_call(
        functools.partial(kernel, n_dp, n_seq),
        out_shape=(
            jax.ShapeDtypeStruct((slots, rows, columns), bf16),
            jax.ShapeDtypeStruct((depth, columns), f32),
        ),
        in_specs=[ANY, ANY, ANY, ANY, VMEM, VMEM, SMEM, SMEM, SMEM],
        out_specs=[VMEM, VMEM],
        scratch_shapes=[
            pltpu.VMEM((slots, rows, features), bf16),
            pltpu.VMEM((square, square), bf16),
            pltpu.VMEM((n_seq, slots, rows, width), bf16),
            pltpu.VMEM((slots, length, width), bf16),
            pltpu.VMEM((width, columns), bf16),
            pltpu.VMEM((n_seq, slots, rows), jnp.int32),
            pltpu.VMEM((length, wide), bf16),
            pltpu.VMEM((length, wide), bf16),
            pltpu.VMEM((length, HD), bf16),
            pltpu.VMEM((length, HD), bf16),
            pltpu.VMEM((heads, triangle, TILE), f32),
            pltpu.VMEM((slots, 2, half, columns), bf16),
            pltpu.VMEM((slots, half, columns), bf16),
            pltpu.VMEM((slots, half, columns), bf16),
            pltpu.VMEM((chips, half, HD), bf16),
            pltpu.VMEM((length, HD), f32),
            pltpu.VMEM((half, HD), bf16),
            pltpu.VMEM((half, HD), bf16),
            pltpu.VMEM((n_seq, half, HD), bf16),
            pltpu.VMEM((length, HD), f32),
            pltpu.VMEM((half, HD), bf16),
            pltpu.VMEM((half, HD), bf16),
            pltpu.VMEM((chips, rows, HD), bf16),
            pltpu.VMEM((slots, rows, columns), bf16),
            pltpu.VMEM((2, rows, columns), bf16),
            pltpu.VMEM((2, rows, columns), bf16),
            pltpu.VMEM((share // HD, HD, columns), bf16),
            pltpu.VMEM((share // HD, HD, columns), bf16),
            pltpu.VMEM((share // HD, HD, columns), f32),
            pltpu.VMEM((n_dp // 2, depth, columns), bf16),
            pltpu.VMEM((n_dp // 2, depth, columns), bf16),
        ]
        + [dma((n_seq,))] * 10
        + [dma((n_dp,))] * 2
        + [dma((2,))] * 2
        + [dma((chips,))] * 8
        + [dma((2,))] * 4
        + [dma((n_dp // 2,))] * 2
        + [dma((3,))] * 2
        + [dma((9,))],
        compiler_params=pltpu.CompilerParams(
            collective_id=0, has_side_effects=True, vmem_limit_bytes=60 << 20
        ),
        name="backward",
    )(
        hidden, queries, keys, upstream, w_value, segment_ids, response_lengths,
        advantages.astype(f32), move_plan.T,
    )


def solution(mesh):
    placed = (
        P("dp", "seq", None),
        P("dp", "seq", None),
        P("dp", "seq", None),
        P("dp", "seq", None),
        P(("dp", "seq"), None),
        P("dp", "seq"),
        P("dp", None),
        P("dp", None),
        P(),
    )
    return jax.shard_map(
        on_device,
        mesh=mesh,
        in_specs=placed,
        out_specs=(P("dp", "seq", None), P(("dp", "seq"), None)),
        check_vma=False,
    )
```

```python
import functools

import jax
import jax.numpy as jnp
from jax import lax
from jax.experimental import pallas as pl
from jax.experimental.pallas import tpu as pltpu
from jax.sharding import PartitionSpec as P

KVH = 4
HD = 128
TILE = 256
MESH = pl.DeviceIdType.MESH
ANY = pl.BlockSpec(memory_space=pl.ANY)
VMEM = pl.BlockSpec(memory_space=pltpu.VMEM)
SMEM = pl.BlockSpec(memory_space=pltpu.SMEM)
OVER_LAST = (((1,), (1,)), ((), ()))
OVER_FIRST = (((0,), (0,)), ((), ()))


def remote(src, dst, send_sem, recv_sem, rank, place):
    return pltpu.make_async_remote_copy(
        src_ref=src,
        dst_ref=dst,
        send_sem=send_sem,
        recv_sem=recv_sem,
        device_id=(rank, place),
        device_id_type=MESH,
    )


def each(low, high, body):
    def step(m, carry):
        body(m)
        return carry

    lax.fori_loop(low, high, step, 0)


class Copies:
    def __init__(self):
        self.groups = {}
        self.landed = set()

    def add(self, name, low, high, make):
        self.groups[name] = (low, high, make)

    def start(self, name, low, high, make):
        self.add(name, low, high, make)
        each(low, high, lambda m: make(m).start())

    def arrive(self, name):
        low, high, make = self.groups[name]
        self.landed.add(name)
        each(low, high, lambda m: make(m).wait_recv())

    def settle(self, *names):
        for name in names:
            low, high, make = self.groups.pop(name)
            each(low, high, lambda m: make(m).wait_send())

    def finish(self):
        self.settle(*self.groups)


def greet(n_dp, n_seq, rank, place):
    barrier = pltpu.get_barrier_semaphore()

    def along_seq(m):
        pl.semaphore_signal(
            barrier, inc=1, device_id=(rank, lax.rem(place + m, n_seq)), device_id_type=MESH
        )

    def along_dp(m):
        pl.semaphore_signal(
            barrier, inc=1, device_id=(lax.rem(rank + m, n_dp), place), device_id_type=MESH
        )

    each(1, n_seq, along_seq)
    each(1, n_dp, along_dp)
    pl.semaphore_wait(barrier, n_seq + n_dp - 2)


def aligned(index, size):
    return pl.ds(pl.multiple_of(index * size, size), size)


def kernel(
    n_dp, n_seq, hidden, queries, keys, upstream, w_value, segs, lengths, gains, plan,
    key_out, weight_out,
    rows_in, perm, y, x, wg, seg, q, u, k, v, probs,
    part, other, red, rs, dv_sum, dv_give, dv_got, vg, dk_sum, dk_own,
    kgs, kg, give, got, dw_far, dw_came, dw_near, dw_own, dw_got,
    s_send, s_recv, k_send, k_recv, q_send, q_recv, u_send, u_recv, o_send, o_recv, x_send, x_recv,
    w_send, w_recv, e_send, e_recv, p_send, p_recv, r_send, r_recv, a_send, a_recv, f_send, f_recv,
    t_send, t_recv, y_send, y_recv, z_send, z_recv,
    c_send, c_recv, local,
):
    rank, place = lax.axis_index("dp"), lax.axis_index("seq")
    rows = queries.shape[1]
    length = rows * n_seq
    half = length // 2
    wide = q.shape[1]
    per_core = wide // HD
    chips = n_seq // 2
    core, chip = lax.rem(place, 2), place // 2
    sibling = place + 1 - 2 * core
    slot, head = chip // KVH, lax.rem(chip, KVH)
    depth = w_value.shape[0]
    n_z = n_dp // 2
    lane, side = lax.rem(rank, n_z), rank // n_z
    f32, bf16 = jnp.float32, jnp.bfloat16
    scale = HD ** (-0.5)

    copies = Copies()
    load = pltpu.make_async_copy(hidden, rows_in, local.at[0])
    load.start()
    greet(n_dp, n_seq, rank, place)

    def s_copy(m):
        peer = lax.rem(place + m, n_seq)
        return remote(segs, seg.at[place], s_send.at[m], s_recv.at[m], rank, peer)

    def k_part(peer):
        return keys.at[peer // (2 * KVH), :, aligned(lax.rem(peer // 2, KVH), HD)]

    def k_copy(m):
        peer = 2 * lax.rem(chip + m, chips) + core
        return remote(k_part(peer), k.at[aligned(place, rows)], k_send.at[m], k_recv.at[m], rank, peer)

    def k_pass(n):
        origin = 2 * n + core
        return remote(
            k.at[aligned(origin, rows)], k.at[aligned(origin, rows)], p_send.at[n], p_recv.at[n], rank, sibling
        )

    def head_part(array, peer):
        return array.at[peer // (2 * KVH), :, aligned(lax.rem(peer, 2 * KVH), wide)]

    def q_copy(m):
        peer = lax.rem(place + m, n_seq)
        return remote(head_part(queries, peer), q.at[aligned(place, rows)], q_send.at[m], q_recv.at[m], rank, peer)

    def u_copy(m):
        peer = lax.rem(place + m, n_seq)
        return remote(head_part(upstream, peer), u.at[aligned(place, rows)], u_send.at[m], u_recv.at[m], rank, peer)

    def w_copy(m):
        peer = lax.rem(rank + m, n_dp)
        return remote(w_value, wg.at[aligned(rank, depth)], w_send.at[m], w_recv.at[m], peer, place)

    def x_copy(m):
        peer = lax.rem(place + m, n_seq)
        n = m // n_seq
        peer = lax.rem(place + m, n_seq)
        return remote(y.at[n, peer], x.at[n, aligned(place, rows), :], x_send.at[m], x_recv.at[m], rank, peer)

    own = [
        pltpu.make_async_copy(segs, seg.at[place], local.at[1]),
        pltpu.make_async_copy(k_part(place), k.at[aligned(place, rows)], local.at[2]),
        pltpu.make_async_copy(head_part(queries, place), q.at[aligned(place, rows)], local.at[3]),
        pltpu.make_async_copy(head_part(upstream, place), u.at[aligned(place, rows)], local.at[4]),
        pltpu.make_async_copy(w_value, wg.at[aligned(rank, depth)], local.at[5]),
    ]

    def send_keys():
        copies.start("s", 1, n_seq, s_copy)
        copies.start("k", 1, chips, k_copy)

    def send_queries():
        copies.start("q", 1, n_seq, q_copy)

    def send_upstream():
        copies.start("u", 1, n_seq, u_copy)

    def send_weights():
        copies.start("w", 1, n_dp, w_copy)
        for copy in own:
            copy.start()

    own_x = [
        pltpu.make_async_copy(y.at[n, place], x.at[n, aligned(place, rows), :], local.at[6 + n]) for n in range(2)
    ]
    runs = HD // depth

    def regroup():
        size = runs * HD
        i = lax.broadcasted_iota(jnp.int32, (size, size), 0)
        j = lax.broadcasted_iota(jnp.int32, (size, size), 1)
        to = ((i // depth) % runs) * HD + (i // HD) * depth + i % depth
        perm[...] = jnp.where(j == to, 1.0, 0.0).astype(bf16)
        halves = n_seq // runs
        blocks = n_dp // runs
        load.wait()
        for part_of in range(halves):
            for n in range(2):
                stacked = jnp.concatenate(
                    [
                        jnp.concatenate(
                            [
                                rows_in[n, :, t * HD : (t + 1) * HD]
                                for t in range(b * runs * halves + part_of, (b + 1) * runs * halves, halves)
                            ],
                            1,
                        )
                        for b in range(blocks)
                    ],
                    0,
                )
                regrouped = jnp.dot(stacked, perm[...], preferred_element_type=f32).astype(bf16)
                for b in range(blocks):
                    for a in range(runs):
                        y[n, part_of * runs + a, :, b * HD : (b + 1) * HD] = regrouped[
                            b * rows : (b + 1) * rows, a * HD : (a + 1) * HD
                        ]
        for copy in own:
            copy.wait()

    def send_hidden(n):
        copies.start(("x", n), n * n_seq + 1, (n + 1) * n_seq, x_copy)
        own_x[n].start()

    def parts_of(block):
        return block * TILE, (block + 1) * TILE, TILE * block * (block + 1) // 2

    def find_cut():
        return length - jnp.where(slot == 0, jnp.sum(seg[:, 0, :]), jnp.sum(seg[:, 1, :]))

    def make_probs():
        for name in "skq":
            copies.arrive(name)
            if name == "k":
                copies.start("p", 0, chips, k_pass)
        send_hidden(1)
        copies.arrive("p")
        cut = find_cut()

        def of_head(h):
            lanes = aligned(h, HD)
            for block in range(length // TILE):
                at, seen, offset = parts_of(block)
                scores = lax.dot_general(k[:seen], q[at:seen, lanes], OVER_LAST, preferred_element_type=f32)
                j = lax.broadcasted_iota(jnp.int32, (seen, TILE), 0)
                i = lax.broadcasted_iota(jnp.int32, (1, TILE), 1) + at
                least = jnp.where(i >= cut, cut, 0)
                scores = jnp.where((j >= least) & (j <= i), scores, f32(-1e30))
                highest = jnp.max(scores, 0, keepdims=True)
                weighted = jnp.exp2((scores - highest) * (scale * 1.4426950408889634))
                probs[h, offset : offset + seen] = weighted * (1.0 / jnp.sum(weighted, 0, keepdims=True))

        each(0, per_core, of_head)

    dv_swap = remote(dv_give, dv_got, c_send.at[0], c_recv.at[0], rank, sibling)

    def make_value_grads():
        copies.arrive("u")
        cut = find_cut()
        position = lax.broadcasted_iota(jnp.int32, (length, HD), 0)
        second = position >= cut
        last = jnp.where(second, length - 1, cut - 1)
        sampled = jnp.where(second, lengths[slot, 1], lengths[slot, 0])
        table = gains[...].astype(f32)
        table = jnp.where(slot == 0, table[0:1], table[1:2])
        gain = jnp.where(second, table[0:1, 1:2], table[0:1, 0:1])
        weight = jnp.where(last - position < sampled, gain, f32(0.0))
        for h in range(per_core):
            lanes = slice(h * HD, (h + 1) * HD)
            u[:, lanes] = (u[:, lanes].astype(f32) * weight).astype(bf16)
        dv_sum[...] = jnp.zeros_like(dv_sum)

        def of_head(h):
            lanes = aligned(h, HD)
            for block in range(length // TILE):
                at, seen, offset = parts_of(block)
                dv_sum[:seen] += jnp.dot(
                    probs[h, offset : offset + seen].astype(bf16), u[at:seen, lanes], preferred_element_type=f32
                )

        each(0, per_core, of_head)
        dv_give[...] = dv_sum[aligned(1 - core, half)].astype(bf16)
        copies.start("dv_swap", 0, 1, lambda m: dv_swap)

    def a_copy(m):
        peer = lax.rem(chip + m, chips)
        return remote(vg.at[place], vg.at[place], a_send.at[m], a_recv.at[m], rank, 2 * peer + core)

    def f_copy(m):
        origin = 2 * lax.rem(chip - m + chips, chips) + core
        return remote(vg.at[origin], vg.at[origin], f_send.at[m], f_recv.at[m], rank, sibling)

    def send_value_grads():
        copies.arrive("dv_swap")
        vg[place] = (dv_sum[aligned(core, half)] + dv_got[...].astype(f32)).astype(bf16)
        copies.start("a", 1, chips, a_copy)
        f_copy(0).start()
        copies.add("f", 0, chips, f_copy)

    def forward_value_grads():
        def forward(m):
            a_copy(m).wait_recv()
            f_copy(m).start()

        each(1, chips, forward)
        copies.landed.add("a")

    def project(n, which):
        part[n, which] = jnp.dot(x[n, aligned(which, half), :], wg[...], preferred_element_type=f32).astype(bf16)

    def e_copy(n):
        return remote(part.at[n, 1 - core], other.at[n], e_send.at[n], e_recv.at[n], rank, sibling)

    def project_values(n):
        if n == 0:
            copies.arrive("w")
        own_x[n].wait()
        copies.arrive(("x", n))
        project(n, 1 - core)
        copies.start(("e", n), n, n + 1, e_copy)
        project(n, core)

    def r_copy(m):
        peer = lax.rem(chip + m, chips)
        return remote(
            red.at[peer // KVH, :, aligned(lax.rem(peer, KVH), HD)], rs.at[m],
            r_send.at[m], r_recv.at[m], rank, 2 * peer + core,
        )

    own_r = pltpu.make_async_copy(red.at[slot, :, aligned(head, HD)], rs.at[0], local.at[8])

    def send_partials():
        for n in range(2):
            copies.arrive(("e", n))
            red[n] = (part[n, core].astype(f32) + other[n].astype(f32)).astype(bf16)
        copies.start("r", 1, chips, r_copy)
        own_r.start()

    v_swap = remote(
        v.at[aligned(core, half)], v.at[aligned(core, half)], c_send.at[1], c_recv.at[1], rank, sibling
    )

    def sum_values():
        own_r.wait()
        copies.arrive("r")
        total = rs[0].astype(f32)
        for m in range(1, chips):
            total = total + rs[m].astype(f32)
        v[aligned(core, half)] = total.astype(bf16)
        copies.start("v_swap", 0, 1, lambda m: v_swap)

    def o_copy(m):
        peer = lax.rem(place + m, n_seq)
        return remote(
            dk_own.at[aligned(peer, rows)], kgs.at[core, slot, :, aligned(head, HD)],
            o_send.at[m], o_recv.at[m], rank, peer,
        )

    own_o = pltpu.make_async_copy(
        dk_own.at[aligned(place, rows)], kgs.at[core, slot, :, aligned(head, HD)], local.at[9]
    )

    def make_key_grads():
        dk_sum[...] = jnp.zeros_like(dk_sum)
        copies.arrive("v_swap")

        def of_head(h):
            lanes = aligned(h, HD)
            for block in range(length // TILE):
                at, seen, offset = parts_of(block)
                p = probs[h, offset : offset + seen]
                dprobs = lax.dot_general(v[:seen], u[at:seen, lanes], OVER_LAST, preferred_element_type=f32)
                dscores = p * (dprobs - jnp.sum(p * dprobs, 0, keepdims=True))
                dk_sum[:seen] += jnp.dot(dscores.astype(bf16), q[at:seen, lanes], preferred_element_type=f32)

        each(0, per_core, of_head)
        dk_own[...] = (dk_sum[...] * scale).astype(bf16)
        copies.start("o", 1, n_seq, o_copy)
        own_o.start()

    def trade(section):
        low = lax.rem(rank // (1 << section), 2)
        partner = rank + (1 << section) * (1 - 2 * low)
        return remote(
            give.at[section], got.at[section], t_send.at[section], t_recv.at[section], partner, place
        )

    def chosen(section):
        return jnp.full(kg.shape[1:], plan[section, rank], jnp.int32)

    def offer(section):
        first, second = kg[0].astype(f32), kg[1].astype(f32)
        give[section] = jnp.where(chosen(section) == 1, second, first).astype(bf16)
        copies.start(("t", section), section, section + 1, trade)

    def accept(section):
        copies.arrive(("t", section))
        giving = chosen(section)
        arrived = got[section].astype(f32)
        for n in range(2):
            kg[n] = jnp.where(giving == n, arrived, kg[n].astype(f32)).astype(bf16)

    def first_trade():
        own_o.wait()
        copies.arrive("o")
        kg[...] = (kgs[0].astype(f32) + kgs[1].astype(f32)).astype(bf16)
        offer(0)

    def second_trade():
        accept(0)
        offer(1)

    def end_trade():
        accept(1)
        key_out[...] = kg[...]

    def weight_terms(column, count):
        total = None
        for n in range(2):
            for which in range(2):
                grads = jnp.concatenate([vg[(n * KVH + g) * 2 + which] for g in range(KVH)], 1)
                term = lax.dot_general(
                    x[n, which * half : (which + 1) * half, pl.ds(pl.multiple_of(column, HD), count)], grads,
                    OVER_FIRST, preferred_element_type=f32,
                )
                total = term if total is None else total + term
        return total

    share = n_z * depth
    pieces, piece = dw_far.shape[0], dw_far.shape[2]

    def y_copy(n):
        return remote(
            dw_far.at[n], dw_came.at[n], y_send.at[n], y_recv.at[n], lane + n_z * (1 - side), place
        )

    def make_weight_grads():
        copies.arrive("f")

        def far(n):
            terms = weight_terms((1 - side) * share + n * HD, HD).astype(bf16)
            for c in range(pieces):
                dw_far[c, aligned(n, HD)] = terms[:, c * piece : (c + 1) * piece]

        def near(n):
            dw_near[aligned(n, HD)] = weight_terms(side * share + n * HD, HD)

        each(0, share // HD, far)
        copies.start("y", 0, pieces, y_copy)
        each(0, share // HD, near)

    def z_copy(m):
        to_lane = lax.rem(lane + m, n_z)
        return remote(
            dw_own.at[m // n_z, to_lane], dw_got.at[m], z_send.at[m], z_recv.at[m], to_lane + n_z * side, place
        )

    def send_weight_grads():
        for c in range(pieces):
            y_copy(c).wait_recv()
            summed = (dw_near[:, c * piece : (c + 1) * piece] + dw_came[c].astype(f32)).astype(bf16)
            dw_own[c] = summed.reshape(n_z, depth, piece)
            copies.start(("z", c), c * n_z + 1, (c + 1) * n_z, z_copy)
        copies.landed.add("y")

    def sum_weight_grads():
        for c in range(pieces):
            copies.arrive(("z", c))
            total = dw_own[c, lane].astype(f32)
            for m in range(c * n_z + 1, (c + 1) * n_z):
                total = total + dw_got[m].astype(f32)
            weight_out[:, c * piece : (c + 1) * piece] = total

    send_keys()
    send_queries()
    send_upstream()
    send_weights()
    regroup()
    send_hidden(0)
    make_probs()
    make_value_grads()
    project_values(0)
    send_value_grads()
    project_values(1)
    forward_value_grads()
    send_partials()
    copies.settle("s", "k", "p", "q", "u", "w", ("x", 0), ("x", 1), ("e", 0), ("e", 1))
    make_weight_grads()
    sum_values()
    send_weight_grads()
    make_key_grads()
    first_trade()
    copies.settle("a", "f", "r", "y", "dv_swap", "v_swap", "o")
    second_trade()
    end_trade()
    sum_weight_grads()
    copies.finish()


def on_device(
    hidden, queries, keys, upstream, w_value, segment_ids, response_lengths, advantages, move_plan
):
    n_dp, n_seq = lax.axis_size("dp"), lax.axis_size("seq")
    slots, rows, features = hidden.shape
    length = rows * n_seq
    half = length // 2
    chips = n_seq // 2
    wide = queries.shape[2] * slots // n_seq
    heads = wide // HD
    depth, columns = w_value.shape
    width = depth * n_dp
    share = width // 2
    bf16, f32 = jnp.bfloat16, jnp.float32
    square = (HD // depth) * HD
    tiles = length // TILE
    triangle = TILE * tiles * (tiles + 1) // 2
    dma = pltpu.SemaphoreType.DMA
    return pl.pallas_call(
        functools.partial(kernel, n_dp, n_seq),
        out_shape=(
            jax.ShapeDtypeStruct((slots, rows, columns), bf16),
            jax.ShapeDtypeStruct((depth, columns), f32),
        ),
        in_specs=[ANY, ANY, ANY, ANY, VMEM, VMEM, SMEM, VMEM, SMEM],
        out_specs=[VMEM, VMEM],
        scratch_shapes=[
            pltpu.VMEM((slots, rows, features), bf16),
            pltpu.VMEM((square, square), bf16),
            pltpu.VMEM((slots, n_seq, rows, width), bf16),
            pltpu.VMEM((slots, length, width), bf16),
            pltpu.VMEM((width, columns), bf16),
            pltpu.VMEM((n_seq, slots, rows), jnp.int32),
            pltpu.VMEM((length, wide), bf16),
            pltpu.VMEM((length, wide), bf16),
            pltpu.VMEM((length, HD), bf16),
            pltpu.VMEM((length, HD), bf16),
            pltpu.VMEM((heads, triangle, TILE), f32),
            pltpu.VMEM((slots, 2, half, columns), bf16),
            pltpu.VMEM((slots, half, columns), bf16),
            pltpu.VMEM((slots, half, columns), bf16),
            pltpu.VMEM((chips, half, HD), bf16),
            pltpu.VMEM((length, HD), f32),
            pltpu.VMEM((half, HD), bf16),
            pltpu.VMEM((half, HD), bf16),
            pltpu.VMEM((n_seq, half, HD), bf16),
            pltpu.VMEM((length, HD), f32),
            pltpu.VMEM((length, HD), bf16),
            pltpu.VMEM((2, slots, rows, columns), bf16),
            pltpu.VMEM((slots, rows, columns), bf16),
            pltpu.VMEM((2, rows, columns), bf16),
            pltpu.VMEM((2, rows, columns), bf16),
            pltpu.VMEM((2, share, columns // 2), bf16),
            pltpu.VMEM((2, share, columns // 2), bf16),
            pltpu.VMEM((share, columns), f32),
            pltpu.VMEM((2, n_dp // 2, depth, columns // 2), bf16),
            pltpu.VMEM((n_dp, depth, columns // 2), bf16),
        ]
        + [dma((n_seq,))] * 10 + [dma((2 * n_seq,))] * 2
        + [dma((n_dp,))] * 2
        + [dma((2,))] * 2
        + [dma((chips,))] * 8
        + [dma((2,))] * 4
        + [dma((n_dp,))] * 2
        + [dma((2,))] * 2
        + [dma((10,))],
        compiler_params=pltpu.CompilerParams(
            collective_id=0, has_side_effects=True, vmem_limit_bytes=60 << 20
        ),
        name="backward",
    )(
        hidden, queries, keys, upstream, w_value, segment_ids, response_lengths,
        advantages, move_plan.T,
    )


def solution(mesh):
    placed = (
        P("dp", "seq", None),
        P("dp", "seq", None),
        P("dp", "seq", None),
        P("dp", "seq", None),
        P(("dp", "seq"), None),
        P("dp", "seq"),
        P("dp", None),
        P("dp", None),
        P(),
    )
    return jax.shard_map(
        on_device,
        mesh=mesh,
        in_specs=placed,
        out_specs=(P("dp", "seq", None), P(("dp", "seq"), None)),
        check_vma=False,
    )
```

```python
import functools

import jax
import jax.numpy as jnp
from jax import lax
from jax.experimental import pallas as pl
from jax.experimental.pallas import tpu as pltpu
from jax.sharding import PartitionSpec as P

KVH = 4
HD = 128
TILE = 256
MESH = pl.DeviceIdType.MESH
ANY = pl.BlockSpec(memory_space=pl.ANY)
VMEM = pl.BlockSpec(memory_space=pltpu.VMEM)
SMEM = pl.BlockSpec(memory_space=pltpu.SMEM)
OVER_LAST = (((1,), (1,)), ((), ()))
OVER_FIRST = (((0,), (0,)), ((), ()))


def remote(src, dst, send_sem, recv_sem, rank, place):
    return pltpu.make_async_remote_copy(
        src_ref=src,
        dst_ref=dst,
        send_sem=send_sem,
        recv_sem=recv_sem,
        device_id=(rank, place),
        device_id_type=MESH,
    )


def each(low, high, body):
    def step(m, carry):
        body(m)
        return carry

    lax.fori_loop(low, high, step, 0)


class Copies:
    def __init__(self):
        self.groups = {}
        self.landed = set()

    def add(self, name, low, high, make):
        self.groups[name] = (low, high, make)

    def start(self, name, low, high, make):
        self.add(name, low, high, make)
        each(low, high, lambda m: make(m).start())

    def arrive(self, name):
        low, high, make = self.groups[name]
        self.landed.add(name)
        each(low, high, lambda m: make(m).wait_recv())

    def settle(self, *names):
        for name in names:
            low, high, make = self.groups.pop(name)
            each(low, high, lambda m: make(m).wait_send())

    def finish(self):
        self.settle(*self.groups)


def greet(n_dp, n_seq, rank, place):
    barrier = pltpu.get_barrier_semaphore()

    def along_seq(m):
        pl.semaphore_signal(
            barrier, inc=1, device_id=(rank, lax.rem(place + m, n_seq)), device_id_type=MESH
        )

    def along_dp(m):
        pl.semaphore_signal(
            barrier, inc=1, device_id=(lax.rem(rank + m, n_dp), place), device_id_type=MESH
        )

    each(1, n_seq, along_seq)
    each(1, n_dp, along_dp)
    pl.semaphore_wait(barrier, n_seq + n_dp - 2)


def aligned(index, size):
    return pl.ds(pl.multiple_of(index * size, size), size)


def kernel(
    n_dp, n_seq, hidden, queries, keys, upstream, w_value, segs, lengths, gains, plan,
    key_out, weight_out,
    rows_in, perm, y, x, w_pair, wg, seg, q, u, k, v, probs,
    part, other, red, rs, dv_sum, dv_give, dv_got, vg, dk_sum, dk_own,
    kgs, kg, give, got, dw_far, dw_came, dw_near, dw_own, dw_got,
    s_send, s_recv, k_send, k_recv, q_send, q_recv, u_send, u_recv, o_send, o_recv, x_send, x_recv,
    w_send, w_recv, e_send, e_recv, p_send, p_recv, r_send, r_recv, a_send, a_recv, f_send, f_recv,
    t_send, t_recv, y_send, y_recv, z_send, z_recv,
    c_send, c_recv, local, b_send, b_recv,
):
    rank, place = lax.axis_index("dp"), lax.axis_index("seq")
    rows = queries.shape[1]
    length = rows * n_seq
    half = length // 2
    wide = q.shape[1]
    per_core = wide // HD
    chips = n_seq // 2
    core, chip = lax.rem(place, 2), place // 2
    sibling = place + 1 - 2 * core
    slot, head = chip // KVH, lax.rem(chip, KVH)
    depth = w_value.shape[0]
    n_z = n_dp // 2
    width, columns = depth * n_dp, w_value.shape[1]
    lane, side = lax.rem(rank, n_z), rank // n_z
    f32, bf16 = jnp.float32, jnp.bfloat16
    scale = HD ** (-0.5)

    copies = Copies()
    load = pltpu.make_async_copy(hidden, rows_in, local.at[0])
    load.start()
    greet(n_dp, n_seq, rank, place)

    def s_copy(m):
        peer = lax.rem(place + m, n_seq)
        return remote(segs, seg.at[place], s_send.at[m], s_recv.at[m], rank, peer)

    def k_part(peer):
        return keys.at[peer // (2 * KVH), :, aligned(lax.rem(peer // 2, KVH), HD)]

    def k_copy(m):
        peer = 2 * lax.rem(chip + m, chips) + core
        return remote(k_part(peer), k.at[aligned(place, rows)], k_send.at[m], k_recv.at[m], rank, peer)

    def k_pass(n):
        origin = 2 * n + core
        return remote(
            k.at[aligned(origin, rows)], k.at[aligned(origin, rows)], p_send.at[n], p_recv.at[n], rank, sibling
        )

    def head_part(array, peer):
        return array.at[peer // (2 * KVH), :, aligned(lax.rem(peer, 2 * KVH), wide)]

    def q_copy(m):
        peer = lax.rem(place + m, n_seq)
        return remote(head_part(queries, peer), q.at[aligned(place, rows)], q_send.at[m], q_recv.at[m], rank, peer)

    def u_copy(m):
        peer = lax.rem(place + m, n_seq)
        return remote(head_part(upstream, peer), u.at[aligned(place, rows)], u_send.at[m], u_recv.at[m], rank, peer)

    def b_copy(n):
        return remote(w_value, w_pair.at[side], b_send.at[n], b_recv.at[n], lane + n_z * (1 - side), place)

    def w_copy(m):
        peer = lax.rem(lane + m, n_z) + n_z * side
        return remote(w_pair, wg.at[:, lane], w_send.at[m], w_recv.at[m], peer, place)

    def x_copy(m):
        peer = lax.rem(place + m, n_seq)
        n = m // n_seq
        peer = lax.rem(place + m, n_seq)
        return remote(y.at[n, peer], x.at[n, aligned(place, rows), :], x_send.at[m], x_recv.at[m], rank, peer)

    own = [
        pltpu.make_async_copy(segs, seg.at[place], local.at[1]),
        pltpu.make_async_copy(k_part(place), k.at[aligned(place, rows)], local.at[2]),
        pltpu.make_async_copy(head_part(queries, place), q.at[aligned(place, rows)], local.at[3]),
        pltpu.make_async_copy(head_part(upstream, place), u.at[aligned(place, rows)], local.at[4]),
        pltpu.make_async_copy(w_value, w_pair.at[side], local.at[5]),
    ]

    def send_keys():
        copies.start("s", 1, n_seq, s_copy)
        copies.start("k", 1, chips, k_copy)

    def send_queries():
        copies.start("q", 1, n_seq, q_copy)

    def send_upstream():
        copies.start("u", 1, n_seq, u_copy)

    own_w = pltpu.make_async_copy(w_pair, wg.at[:, lane], local.at[10])

    def send_weights():
        copies.start("b", 0, 1, b_copy)
        for copy in own:
            copy.start()

    own_x = [
        pltpu.make_async_copy(y.at[n, place], x.at[n, aligned(place, rows), :], local.at[6 + n]) for n in range(2)
    ]
    runs = HD // depth

    def regroup():
        size = runs * HD
        i = lax.broadcasted_iota(jnp.int32, (size, size), 0)
        j = lax.broadcasted_iota(jnp.int32, (size, size), 1)
        to = ((i // depth) % runs) * HD + (i // HD) * depth + i % depth
        perm[...] = jnp.where(j == to, 1.0, 0.0).astype(bf16)
        halves = n_seq // runs
        blocks = n_dp // runs
        load.wait()
        for part_of in range(halves):
            for n in range(2):
                stacked = jnp.concatenate(
                    [
                        jnp.concatenate(
                            [
                                rows_in[n, :, t * HD : (t + 1) * HD]
                                for t in range(b * runs * halves + part_of, (b + 1) * runs * halves, halves)
                            ],
                            1,
                        )
                        for b in range(blocks)
                    ],
                    0,
                )
                regrouped = jnp.dot(stacked, perm[...], preferred_element_type=f32).astype(bf16)
                for b in range(blocks):
                    for a in range(runs):
                        y[n, part_of * runs + a, :, b * HD : (b + 1) * HD] = regrouped[
                            b * rows : (b + 1) * rows, a * HD : (a + 1) * HD
                        ]
        for copy in own:
            copy.wait()
        copies.arrive("b")
        copies.start("w", 1, n_z, w_copy)
        own_w.start()

    def send_hidden(n):
        copies.start(("x", n), n * n_seq + 1, (n + 1) * n_seq, x_copy)
        own_x[n].start()

    def parts_of(block):
        return block * TILE, (block + 1) * TILE, TILE * block * (block + 1) // 2

    def find_cut():
        return length - jnp.where(slot == 0, jnp.sum(seg[:, 0, :]), jnp.sum(seg[:, 1, :]))

    def make_probs():
        for name in "skq":
            copies.arrive(name)
            if name == "k":
                copies.start("p", 0, chips, k_pass)
        send_hidden(1)
        copies.arrive("p")
        cut = find_cut()

        def of_head(h):
            lanes = aligned(h, HD)
            for block in range(length // TILE):
                at, seen, offset = parts_of(block)
                scores = lax.dot_general(k[:seen], q[at:seen, lanes], OVER_LAST, preferred_element_type=f32)
                j = lax.broadcasted_iota(jnp.int32, (seen, TILE), 0)
                i = lax.broadcasted_iota(jnp.int32, (1, TILE), 1) + at
                least = jnp.where(i >= cut, cut, 0)
                scores = jnp.where((j >= least) & (j <= i), scores, f32(-1e30))
                highest = jnp.max(scores, 0, keepdims=True)
                weighted = jnp.exp2((scores - highest) * (scale * 1.4426950408889634))
                probs[h, offset : offset + seen] = weighted * (1.0 / jnp.sum(weighted, 0, keepdims=True))

        each(0, per_core, of_head)

    dv_swap = remote(dv_give, dv_got, c_send.at[0], c_recv.at[0], rank, sibling)

    def make_value_grads():
        copies.arrive("u")
        cut = find_cut()
        position = lax.broadcasted_iota(jnp.int32, (length, HD), 0)
        second = position >= cut
        last = jnp.where(second, length - 1, cut - 1)
        sampled = jnp.where(second, lengths[slot, 1], lengths[slot, 0])
        table = gains[...].astype(f32)
        table = jnp.where(slot == 0, table[0:1], table[1:2])
        gain = jnp.where(second, table[0:1, 1:2], table[0:1, 0:1])
        weight = jnp.where(last - position < sampled, gain, f32(0.0))
        for h in range(per_core):
            lanes = slice(h * HD, (h + 1) * HD)
            u[:, lanes] = (u[:, lanes].astype(f32) * weight).astype(bf16)
        dv_sum[...] = jnp.zeros_like(dv_sum)

        def of_head(h):
            lanes = aligned(h, HD)
            for block in range(length // TILE):
                at, seen, offset = parts_of(block)
                dv_sum[:seen] += jnp.dot(
                    probs[h, offset : offset + seen].astype(bf16), u[at:seen, lanes], preferred_element_type=f32
                )

        each(0, per_core, of_head)
        dv_give[...] = dv_sum[aligned(1 - core, half)].astype(bf16)
        copies.start("dv_swap", 0, 1, lambda m: dv_swap)

    def a_copy(m):
        peer = lax.rem(chip + m, chips)
        return remote(vg.at[place], vg.at[place], a_send.at[m], a_recv.at[m], rank, 2 * peer + core)

    def f_copy(m):
        origin = 2 * lax.rem(chip - m + chips, chips) + core
        return remote(vg.at[origin], vg.at[origin], f_send.at[m], f_recv.at[m], rank, sibling)

    def send_value_grads():
        copies.arrive("dv_swap")
        vg[place] = (dv_sum[aligned(core, half)] + dv_got[...].astype(f32)).astype(bf16)
        copies.start("a", 1, chips, a_copy)
        f_copy(0).start()
        copies.add("f", 0, chips, f_copy)

    def forward_value_grads():
        def forward(m):
            a_copy(m).wait_recv()
            f_copy(m).start()

        each(1, chips, forward)
        copies.landed.add("a")

    def project(n, which):
        part[n, which] = jnp.dot(x[n, aligned(which, half), :], wg[...].reshape(width, columns), preferred_element_type=f32).astype(bf16)

    def e_copy(n):
        return remote(part.at[n, 1 - core], other.at[n], e_send.at[n], e_recv.at[n], rank, sibling)

    def project_values(n):
        if n == 0:
            copies.arrive("w")
            own_w.wait()
        own_x[n].wait()
        copies.arrive(("x", n))
        project(n, 1 - core)
        copies.start(("e", n), n, n + 1, e_copy)
        project(n, core)

    def r_copy(m):
        peer = lax.rem(chip + m, chips)
        return remote(
            red.at[peer // KVH, :, aligned(lax.rem(peer, KVH), HD)], rs.at[m],
            r_send.at[m], r_recv.at[m], rank, 2 * peer + core,
        )

    own_r = pltpu.make_async_copy(red.at[slot, :, aligned(head, HD)], rs.at[0], local.at[8])

    def send_partials():
        for n in range(2):
            copies.arrive(("e", n))
            red[n] = (part[n, core].astype(f32) + other[n].astype(f32)).astype(bf16)
        copies.start("r", 1, chips, r_copy)
        own_r.start()

    v_swap = remote(
        v.at[aligned(core, half)], v.at[aligned(core, half)], c_send.at[1], c_recv.at[1], rank, sibling
    )

    def sum_values():
        own_r.wait()
        copies.arrive("r")
        total = rs[0].astype(f32)
        for m in range(1, chips):
            total = total + rs[m].astype(f32)
        v[aligned(core, half)] = total.astype(bf16)
        copies.start("v_swap", 0, 1, lambda m: v_swap)

    def o_copy(m):
        peer = lax.rem(place + m, n_seq)
        return remote(
            dk_own.at[aligned(peer, rows)], kgs.at[core, slot, :, aligned(head, HD)],
            o_send.at[m], o_recv.at[m], rank, peer,
        )

    own_o = pltpu.make_async_copy(
        dk_own.at[aligned(place, rows)], kgs.at[core, slot, :, aligned(head, HD)], local.at[9]
    )

    def make_key_grads():
        dk_sum[...] = jnp.zeros_like(dk_sum)
        copies.arrive("v_swap")

        def of_head(h):
            lanes = aligned(h, HD)
            for block in range(length // TILE):
                at, seen, offset = parts_of(block)
                p = probs[h, offset : offset + seen]
                dprobs = lax.dot_general(v[:seen], u[at:seen, lanes], OVER_LAST, preferred_element_type=f32)
                dscores = p * (dprobs - jnp.sum(p * dprobs, 0, keepdims=True))
                dk_sum[:seen] += jnp.dot(dscores.astype(bf16), q[at:seen, lanes], preferred_element_type=f32)

        each(0, per_core, of_head)
        dk_own[...] = (dk_sum[...] * scale).astype(bf16)
        copies.start("o", 1, n_seq, o_copy)
        own_o.start()

    def trade(section):
        low = lax.rem(rank // (1 << section), 2)
        partner = rank + (1 << section) * (1 - 2 * low)
        return remote(
            give.at[section], got.at[section], t_send.at[section], t_recv.at[section], partner, place
        )

    def chosen(section):
        return jnp.full(kg.shape[1:], plan[section, rank], jnp.int32)

    def offer(section):
        first, second = kg[0].astype(f32), kg[1].astype(f32)
        give[section] = jnp.where(chosen(section) == 1, second, first).astype(bf16)
        copies.start(("t", section), section, section + 1, trade)

    def accept(section):
        copies.arrive(("t", section))
        giving = chosen(section)
        arrived = got[section].astype(f32)
        for n in range(2):
            kg[n] = jnp.where(giving == n, arrived, kg[n].astype(f32)).astype(bf16)

    def first_trade():
        own_o.wait()
        copies.arrive("o")
        kg[...] = (kgs[0].astype(f32) + kgs[1].astype(f32)).astype(bf16)
        offer(0)

    def second_trade():
        accept(0)
        offer(1)

    def end_trade():
        accept(1)
        key_out[...] = kg[...]

    def weight_terms(column, count):
        total = None
        for n in range(2):
            for which in range(2):
                grads = jnp.concatenate([vg[(n * KVH + g) * 2 + which] for g in range(KVH)], 1)
                term = lax.dot_general(
                    x[n, which * half : (which + 1) * half, pl.ds(pl.multiple_of(column, HD), count)], grads,
                    OVER_FIRST, preferred_element_type=f32,
                )
                total = term if total is None else total + term
        return total

    share = n_z * depth
    pieces, piece = dw_far.shape[0], dw_far.shape[2]

    def y_copy(n):
        return remote(
            dw_far.at[n], dw_came.at[n], y_send.at[n], y_recv.at[n], lane + n_z * (1 - side), place
        )

    def make_weight_grads():
        copies.arrive("f")

        def far(n):
            terms = weight_terms((1 - side) * share + n * HD, HD).astype(bf16)
            for c in range(pieces):
                dw_far[c, aligned(n, HD)] = terms[:, c * piece : (c + 1) * piece]

        def near(n):
            dw_near[aligned(n, HD)] = weight_terms(side * share + n * HD, HD)

        each(0, share // HD, far)
        copies.start("y", 0, pieces, y_copy)
        each(0, share // HD, near)

    def z_copy(m):
        to_lane = lax.rem(lane + m, n_z)
        return remote(
            dw_own.at[m // n_z, to_lane], dw_got.at[m], z_send.at[m], z_recv.at[m], to_lane + n_z * side, place
        )

    def send_weight_grads():
        for c in range(pieces):
            y_copy(c).wait_recv()
            summed = (dw_near[:, c * piece : (c + 1) * piece] + dw_came[c].astype(f32)).astype(bf16)
            dw_own[c] = summed.reshape(n_z, depth, piece)
            copies.start(("z", c), c * n_z + 1, (c + 1) * n_z, z_copy)
        copies.landed.add("y")

    def sum_weight_grads():
        for c in range(pieces):
            copies.arrive(("z", c))
            total = dw_own[c, lane].astype(f32)
            for m in range(c * n_z + 1, (c + 1) * n_z):
                total = total + dw_got[m].astype(f32)
            weight_out[:, c * piece : (c + 1) * piece] = total

    send_weights()
    send_keys()
    send_queries()
    send_upstream()
    regroup()
    send_hidden(0)
    make_probs()
    make_value_grads()
    send_value_grads()
    project_values(0)
    project_values(1)
    send_partials()
    forward_value_grads()
    copies.settle("s", "k", "p", "q", "u", "b", "w", ("x", 0), ("x", 1), ("e", 0), ("e", 1))
    make_weight_grads()
    sum_values()
    send_weight_grads()
    make_key_grads()
    first_trade()
    copies.settle("a", "f", "r", "y", "dv_swap", "v_swap", "o")
    second_trade()
    end_trade()
    sum_weight_grads()
    copies.finish()


def hand_over(key_ref, weight_ref, key_out, weight_out):
    key_out[...] = key_ref[...]
    weight_out[...] = weight_ref[...]


def on_device(
    hidden, queries, keys, upstream, w_value, segment_ids, response_lengths, advantages, move_plan
):
    n_dp, n_seq = lax.axis_size("dp"), lax.axis_size("seq")
    slots, rows, features = hidden.shape
    length = rows * n_seq
    half = length // 2
    chips = n_seq // 2
    wide = queries.shape[2] * slots // n_seq
    heads = wide // HD
    depth, columns = w_value.shape
    width = depth * n_dp
    share = width // 2
    bf16, f32 = jnp.bfloat16, jnp.float32
    square = (HD // depth) * HD
    tiles = length // TILE
    triangle = TILE * tiles * (tiles + 1) // 2
    dma = pltpu.SemaphoreType.DMA
    key_grads, weight_grads = pl.pallas_call(
        functools.partial(kernel, n_dp, n_seq),
        out_shape=(
            jax.ShapeDtypeStruct((slots, rows, columns), bf16),
            jax.ShapeDtypeStruct((depth, columns), f32),
        ),
        in_specs=[ANY, ANY, ANY, ANY, VMEM, VMEM, SMEM, VMEM, SMEM],
        out_specs=[VMEM, VMEM],
        scratch_shapes=[
            pltpu.VMEM((slots, rows, features), bf16),
            pltpu.VMEM((square, square), bf16),
            pltpu.VMEM((slots, n_seq, rows, width), bf16),
            pltpu.VMEM((slots, length, width), bf16),
            pltpu.VMEM((2, depth, columns), bf16),
            pltpu.VMEM((2, n_dp // 2, depth, columns), bf16),
            pltpu.VMEM((n_seq, slots, rows), jnp.int32),
            pltpu.VMEM((length, wide), bf16),
            pltpu.VMEM((length, wide), bf16),
            pltpu.VMEM((length, HD), bf16),
            pltpu.VMEM((length, HD), bf16),
            pltpu.VMEM((heads, triangle, TILE), f32),
            pltpu.VMEM((slots, 2, half, columns), bf16),
            pltpu.VMEM((slots, half, columns), bf16),
            pltpu.VMEM((slots, half, columns), bf16),
            pltpu.VMEM((chips, half, HD), bf16),
            pltpu.VMEM((length, HD), f32),
            pltpu.VMEM((half, HD), bf16),
            pltpu.VMEM((half, HD), bf16),
            pltpu.VMEM((n_seq, half, HD), bf16),
            pltpu.VMEM((length, HD), f32),
            pltpu.VMEM((length, HD), bf16),
            pltpu.VMEM((2, slots, rows, columns), bf16),
            pltpu.VMEM((slots, rows, columns), bf16),
            pltpu.VMEM((2, rows, columns), bf16),
            pltpu.VMEM((2, rows, columns), bf16),
            pltpu.VMEM((2, share, columns // 2), bf16),
            pltpu.VMEM((2, share, columns // 2), bf16),
            pltpu.VMEM((share, columns), f32),
            pltpu.VMEM((2, n_dp // 2, depth, columns // 2), bf16),
            pltpu.VMEM((n_dp, depth, columns // 2), bf16),
        ]
        + [dma((n_seq,))] * 10 + [dma((2 * n_seq,))] * 2
        + [dma((n_dp,))] * 2
        + [dma((2,))] * 2
        + [dma((chips,))] * 8
        + [dma((2,))] * 4
        + [dma((n_dp,))] * 2
        + [dma((2,))] * 2
        + [dma((11,))] + [dma((1,))] * 2,
        compiler_params=pltpu.CompilerParams(
            collective_id=0, has_side_effects=True, vmem_limit_bytes=60 << 20
        ),
        name="backward",
    )(
        hidden, queries, keys, upstream, w_value, segment_ids, response_lengths,
        advantages, move_plan.T,
    )
    return pl.pallas_call(
        hand_over,
        out_shape=(
            jax.ShapeDtypeStruct(key_grads.shape, key_grads.dtype),
            jax.ShapeDtypeStruct(weight_grads.shape, weight_grads.dtype),
        ),
        in_specs=[VMEM, VMEM],
        out_specs=[VMEM, VMEM],
        name="hand_over",
    )(key_grads, weight_grads)


def solution(mesh):
    placed = (
        P("dp", "seq", None),
        P("dp", "seq", None),
        P("dp", "seq", None),
        P("dp", "seq", None),
        P(("dp", "seq"), None),
        P("dp", "seq"),
        P("dp", None),
        P("dp", None),
        P(),
    )
    return jax.shard_map(
        on_device,
        mesh=mesh,
        in_specs=placed,
        out_specs=(P("dp", "seq", None), P(("dp", "seq"), None)),
        check_vma=False,
    )
```

```python
import functools

import jax
import jax.numpy as jnp
from jax import lax
from jax.experimental import pallas as pl
from jax.experimental.pallas import tpu as pltpu
from jax.sharding import PartitionSpec as P

KVH = 4
HD = 128
TILE = 256
MESH = pl.DeviceIdType.MESH
ANY = pl.BlockSpec(memory_space=pl.ANY)
VMEM = pl.BlockSpec(memory_space=pltpu.VMEM)
SMEM = pl.BlockSpec(memory_space=pltpu.SMEM)
OVER_LAST = (((1,), (1,)), ((), ()))
OVER_FIRST = (((0,), (0,)), ((), ()))


def remote(src, dst, send_sem, recv_sem, rank, place):
    return pltpu.make_async_remote_copy(
        src_ref=src,
        dst_ref=dst,
        send_sem=send_sem,
        recv_sem=recv_sem,
        device_id=(rank, place),
        device_id_type=MESH,
    )


def each(low, high, body):
    def step(m, carry):
        body(m)
        return carry

    lax.fori_loop(low, high, step, 0)


class Copies:
    def __init__(self):
        self.groups = {}
        self.landed = set()

    def add(self, name, low, high, make):
        self.groups[name] = (low, high, make)

    def start(self, name, low, high, make):
        self.add(name, low, high, make)
        each(low, high, lambda m: make(m).start())

    def arrive(self, name):
        low, high, make = self.groups[name]
        self.landed.add(name)
        each(low, high, lambda m: make(m).wait_recv())

    def settle(self, *names):
        for name in names:
            low, high, make = self.groups.pop(name)
            each(low, high, lambda m: make(m).wait_send())

    def finish(self):
        self.settle(*self.groups)


def greet(n_dp, n_seq, rank, place):
    barrier = pltpu.get_barrier_semaphore()

    def along_seq(m):
        pl.semaphore_signal(
            barrier, inc=1, device_id=(rank, lax.rem(place + m, n_seq)), device_id_type=MESH
        )

    def along_dp(m):
        pl.semaphore_signal(
            barrier, inc=1, device_id=(lax.rem(rank + m, n_dp), place), device_id_type=MESH
        )

    each(1, n_seq, along_seq)
    each(1, n_dp, along_dp)
    pl.semaphore_wait(barrier, n_seq + n_dp - 2)


def aligned(index, size):
    return pl.ds(pl.multiple_of(index * size, size), size)


def kernel(
    n_dp, n_seq, hidden, queries, keys, upstream, w_value, segs, lengths, gains, plan,
    key_out, weight_out,
    rows_in, perm, y, x, w_pair, wg, seg, q, u, k, v, probs,
    part, other, red, rs, dv_sum, dv_give, dv_got, vg, dk_sum, dk_own,
    kgs, kg, give, got, dw_far, dw_came, dw_near, dw_own, dw_got,
    s_send, s_recv, k_send, k_recv, q_send, q_recv, u_send, u_recv, o_send, o_recv, x_send, x_recv,
    w_send, w_recv, e_send, e_recv, p_send, p_recv, r_send, r_recv, a_send, a_recv, f_send, f_recv,
    t_send, t_recv, y_send, y_recv, z_send, z_recv,
    c_send, c_recv, local, b_send, b_recv,
):
    rank, place = lax.axis_index("dp"), lax.axis_index("seq")
    rows = queries.shape[1]
    length = rows * n_seq
    half = length // 2
    wide = q.shape[1]
    per_core = wide // HD
    chips = n_seq // 2
    core, chip = lax.rem(place, 2), place // 2
    sibling = place + 1 - 2 * core
    slot, head = chip // KVH, lax.rem(chip, KVH)
    depth = w_value.shape[0]
    n_z = n_dp // 2
    width, columns = depth * n_dp, w_value.shape[1]
    lane, side = lax.rem(rank, n_z), rank // n_z
    f32, bf16 = jnp.float32, jnp.bfloat16
    scale = HD ** (-0.5)

    copies = Copies()
    load = pltpu.make_async_copy(hidden, rows_in, local.at[0])
    load.start()
    greet(n_dp, n_seq, rank, place)

    def s_copy(m):
        peer = lax.rem(place + m, n_seq)
        return remote(segs, seg.at[place], s_send.at[m], s_recv.at[m], rank, peer)

    def k_part(peer):
        return keys.at[peer // (2 * KVH), :, aligned(lax.rem(peer // 2, KVH), HD)]

    def k_copy(m):
        peer = 2 * lax.rem(chip + m, chips) + core
        return remote(k_part(peer), k.at[aligned(place, rows)], k_send.at[m], k_recv.at[m], rank, peer)

    def k_pass(n):
        origin = 2 * n + core
        return remote(
            k.at[aligned(origin, rows)], k.at[aligned(origin, rows)], p_send.at[n], p_recv.at[n], rank, sibling
        )

    def head_part(array, peer):
        return array.at[peer // (2 * KVH), :, aligned(lax.rem(peer, 2 * KVH), wide)]

    def q_copy(m):
        peer = lax.rem(place + m, n_seq)
        return remote(head_part(queries, peer), q.at[aligned(place, rows)], q_send.at[m], q_recv.at[m], rank, peer)

    def u_copy(m):
        peer = lax.rem(place + m, n_seq)
        return remote(head_part(upstream, peer), u.at[aligned(place, rows)], u_send.at[m], u_recv.at[m], rank, peer)

    def b_copy(n):
        return remote(w_value, w_pair.at[side], b_send.at[n], b_recv.at[n], lane + n_z * (1 - side), place)

    def w_copy(m):
        peer = lax.rem(lane + m, n_z) + n_z * side
        return remote(w_pair, wg.at[:, lane], w_send.at[m], w_recv.at[m], peer, place)

    def x_copy(m):
        peer = lax.rem(place + m, n_seq)
        n = m // n_seq
        peer = lax.rem(place + m, n_seq)
        return remote(y.at[n, peer], x.at[n, aligned(place, rows), :], x_send.at[m], x_recv.at[m], rank, peer)

    own = [
        pltpu.make_async_copy(segs, seg.at[place], local.at[1]),
        pltpu.make_async_copy(k_part(place), k.at[aligned(place, rows)], local.at[2]),
        pltpu.make_async_copy(head_part(queries, place), q.at[aligned(place, rows)], local.at[3]),
        pltpu.make_async_copy(head_part(upstream, place), u.at[aligned(place, rows)], local.at[4]),
        pltpu.make_async_copy(w_value, w_pair.at[side], local.at[5]),
    ]

    def send_keys():
        copies.start("s", 1, n_seq, s_copy)
        copies.start("k", 1, chips, k_copy)

    def send_queries():
        copies.start("q", 1, n_seq, q_copy)

    def send_upstream():
        copies.start("u", 1, n_seq, u_copy)

    own_w = pltpu.make_async_copy(w_pair, wg.at[:, lane], local.at[10])

    def send_weights():
        copies.start("b", 0, 1, b_copy)
        for copy in own:
            copy.start()

    own_x = [
        pltpu.make_async_copy(y.at[n, place], x.at[n, aligned(place, rows), :], local.at[6 + n]) for n in range(2)
    ]
    runs = HD // depth

    def regroup():
        size = runs * HD
        i = lax.broadcasted_iota(jnp.int32, (size, size), 0)
        j = lax.broadcasted_iota(jnp.int32, (size, size), 1)
        to = ((i // depth) % runs) * HD + (i // HD) * depth + i % depth
        perm[...] = jnp.where(j == to, 1.0, 0.0).astype(bf16)
        halves = n_seq // runs
        blocks = n_dp // runs
        load.wait()
        for part_of in range(halves):
            for n in range(2):
                stacked = jnp.concatenate(
                    [
                        jnp.concatenate(
                            [
                                rows_in[n, :, t * HD : (t + 1) * HD]
                                for t in range(b * runs * halves + part_of, (b + 1) * runs * halves, halves)
                            ],
                            1,
                        )
                        for b in range(blocks)
                    ],
                    0,
                )
                regrouped = jnp.dot(stacked, perm[...], preferred_element_type=f32).astype(bf16)
                for b in range(blocks):
                    for a in range(runs):
                        y[n, part_of * runs + a, :, b * HD : (b + 1) * HD] = regrouped[
                            b * rows : (b + 1) * rows, a * HD : (a + 1) * HD
                        ]
        for copy in own:
            copy.wait()
        copies.arrive("b")
        copies.start("w", 1, n_z, w_copy)
        own_w.start()

    def send_hidden(n):
        copies.start(("x", n), n * n_seq + 1, (n + 1) * n_seq, x_copy)
        own_x[n].start()

    def parts_of(block):
        return block * TILE, (block + 1) * TILE, TILE * block * (block + 1) // 2

    def find_cut():
        return length - jnp.where(slot == 0, jnp.sum(seg[:, 0, :]), jnp.sum(seg[:, 1, :]))

    def make_probs():
        for name in "skq":
            copies.arrive(name)
            if name == "k":
                copies.start("p", 0, chips, k_pass)
        copies.arrive("p")
        cut = find_cut()

        def of_head(h):
            lanes = aligned(h, HD)
            for block in range(length // TILE):
                at, seen, offset = parts_of(block)
                scores = lax.dot_general(k[:seen], q[at:seen, lanes], OVER_LAST, preferred_element_type=f32)
                j = lax.broadcasted_iota(jnp.int32, (seen, TILE), 0)
                i = lax.broadcasted_iota(jnp.int32, (1, TILE), 1) + at
                least = jnp.where(i >= cut, cut, 0)
                scores = jnp.where((j >= least) & (j <= i), scores, f32(-1e30))
                highest = jnp.max(scores, 0, keepdims=True)
                weighted = jnp.exp2((scores - highest) * (scale * 1.4426950408889634))
                probs[h, offset : offset + seen] = weighted * (1.0 / jnp.sum(weighted, 0, keepdims=True))

        each(0, per_core, of_head)

    dv_swap = remote(dv_give, dv_got, c_send.at[0], c_recv.at[0], rank, sibling)

    def make_value_grads():
        copies.arrive("u")
        cut = find_cut()
        position = lax.broadcasted_iota(jnp.int32, (length, HD), 0)
        second = position >= cut
        last = jnp.where(second, length - 1, cut - 1)
        sampled = jnp.where(second, lengths[slot, 1], lengths[slot, 0])
        table = gains[...].astype(f32)
        table = jnp.where(slot == 0, table[0:1], table[1:2])
        gain = jnp.where(second, table[0:1, 1:2], table[0:1, 0:1])
        weight = jnp.where(last - position < sampled, gain, f32(0.0))
        for h in range(per_core):
            lanes = slice(h * HD, (h + 1) * HD)
            u[:, lanes] = (u[:, lanes].astype(f32) * weight).astype(bf16)
        dv_sum[...] = jnp.zeros_like(dv_sum)

        def of_head(h):
            lanes = aligned(h, HD)
            for block in range(length // TILE):
                at, seen, offset = parts_of(block)
                dv_sum[:seen] += jnp.dot(
                    probs[h, offset : offset + seen].astype(bf16), u[at:seen, lanes], preferred_element_type=f32
                )

        each(0, per_core, of_head)
        dv_give[...] = dv_sum[aligned(1 - core, half)].astype(bf16)
        copies.start("dv_swap", 0, 1, lambda m: dv_swap)

    def a_copy(m):
        peer = lax.rem(chip + m, chips)
        return remote(vg.at[place], vg.at[place], a_send.at[m], a_recv.at[m], rank, 2 * peer + core)

    def f_copy(m):
        origin = 2 * lax.rem(chip - m + chips, chips) + core
        return remote(vg.at[origin], vg.at[origin], f_send.at[m], f_recv.at[m], rank, sibling)

    def send_value_grads():
        copies.arrive("dv_swap")
        vg[place] = (dv_sum[aligned(core, half)] + dv_got[...].astype(f32)).astype(bf16)
        copies.start("a", 1, chips, a_copy)
        f_copy(0).start()
        copies.add("f", 0, chips, f_copy)

    def forward_value_grads():
        def forward(m):
            a_copy(m).wait_recv()
            f_copy(m).start()

        each(1, chips, forward)
        copies.landed.add("a")

    def project(n, which):
        part[n, which] = jnp.dot(x[n, aligned(which, half), :], wg[...].reshape(width, columns), preferred_element_type=f32).astype(bf16)

    def e_copy(n):
        return remote(part.at[n, 1 - core], other.at[n], e_send.at[n], e_recv.at[n], rank, sibling)

    def project_values(n):
        if n == 0:
            copies.arrive("w")
            own_w.wait()
        own_x[n].wait()
        copies.arrive(("x", n))
        project(n, 1 - core)
        copies.start(("e", n), n, n + 1, e_copy)
        project(n, core)

    def r_copy(m):
        peer = lax.rem(chip + m, chips)
        return remote(
            red.at[peer // KVH, :, aligned(lax.rem(peer, KVH), HD)], rs.at[m],
            r_send.at[m], r_recv.at[m], rank, 2 * peer + core,
        )

    own_r = pltpu.make_async_copy(red.at[slot, :, aligned(head, HD)], rs.at[0], local.at[8])

    def send_partials():
        for n in range(2):
            copies.arrive(("e", n))
            red[n] = (part[n, core].astype(f32) + other[n].astype(f32)).astype(bf16)
        copies.start("r", 1, chips, r_copy)
        own_r.start()

    v_swap = remote(
        v.at[aligned(core, half)], v.at[aligned(core, half)], c_send.at[1], c_recv.at[1], rank, sibling
    )

    def sum_values():
        own_r.wait()
        copies.arrive("r")
        total = rs[0].astype(f32)
        for m in range(1, chips):
            total = total + rs[m].astype(f32)
        v[aligned(core, half)] = total.astype(bf16)
        copies.start("v_swap", 0, 1, lambda m: v_swap)

    def o_copy(m):
        peer = lax.rem(place + m, n_seq)
        return remote(
            dk_own.at[aligned(peer, rows)], kgs.at[core, slot, :, aligned(head, HD)],
            o_send.at[m], o_recv.at[m], rank, peer,
        )

    own_o = pltpu.make_async_copy(
        dk_own.at[aligned(place, rows)], kgs.at[core, slot, :, aligned(head, HD)], local.at[9]
    )

    def make_key_grads():
        dk_sum[...] = jnp.zeros_like(dk_sum)
        copies.arrive("v_swap")

        def of_head(h):
            lanes = aligned(h, HD)
            for block in range(length // TILE):
                at, seen, offset = parts_of(block)
                p = probs[h, offset : offset + seen]
                dprobs = lax.dot_general(v[:seen], u[at:seen, lanes], OVER_LAST, preferred_element_type=f32)
                dscores = p * (dprobs - jnp.sum(p * dprobs, 0, keepdims=True))
                dk_sum[:seen] += jnp.dot(dscores.astype(bf16), q[at:seen, lanes], preferred_element_type=f32)

        each(0, per_core, of_head)
        dk_own[...] = (dk_sum[...] * scale).astype(bf16)
        copies.start("o", 1, n_seq, o_copy)
        own_o.start()

    def trade(section):
        low = lax.rem(rank // (1 << section), 2)
        partner = rank + (1 << section) * (1 - 2 * low)
        return remote(
            give.at[section], got.at[section], t_send.at[section], t_recv.at[section], partner, place
        )

    def chosen(section):
        return jnp.full(kg.shape[1:], plan[section, rank], jnp.int32)

    def offer(section):
        first, second = kg[0].astype(f32), kg[1].astype(f32)
        give[section] = jnp.where(chosen(section) == 1, second, first).astype(bf16)
        copies.start(("t", section), section, section + 1, trade)

    def accept(section):
        copies.arrive(("t", section))
        giving = chosen(section)
        arrived = got[section].astype(f32)
        for n in range(2):
            kg[n] = jnp.where(giving == n, arrived, kg[n].astype(f32)).astype(bf16)

    def first_trade():
        own_o.wait()
        copies.arrive("o")
        kg[...] = (kgs[0].astype(f32) + kgs[1].astype(f32)).astype(bf16)
        offer(0)

    def second_trade():
        accept(0)
        offer(1)

    def end_trade():
        accept(1)
        key_out[...] = kg[...]

    def weight_terms(column, count):
        total = None
        for n in range(2):
            for which in range(2):
                grads = jnp.concatenate([vg[(n * KVH + g) * 2 + which] for g in range(KVH)], 1)
                term = lax.dot_general(
                    x[n, which * half : (which + 1) * half, pl.ds(pl.multiple_of(column, HD), count)], grads,
                    OVER_FIRST, preferred_element_type=f32,
                )
                total = term if total is None else total + term
        return total

    share = n_z * depth
    pieces, piece = dw_far.shape[0], dw_far.shape[2]

    def y_copy(n):
        return remote(
            dw_far.at[n], dw_came.at[n], y_send.at[n], y_recv.at[n], lane + n_z * (1 - side), place
        )

    def make_weight_grads():
        copies.arrive("f")

        def far(n):
            terms = weight_terms((1 - side) * share + n * HD, HD).astype(bf16)
            for c in range(pieces):
                dw_far[c, aligned(n, HD)] = terms[:, c * piece : (c + 1) * piece]

        def near(n):
            dw_near[aligned(n, HD)] = weight_terms(side * share + n * HD, HD)

        each(0, share // HD, far)
        copies.start("y", 0, pieces, y_copy)
        each(0, share // HD, near)

    def z_copy(m):
        to_lane = lax.rem(lane + m, n_z)
        return remote(
            dw_own.at[m // n_z, to_lane], dw_got.at[m], z_send.at[m], z_recv.at[m], to_lane + n_z * side, place
        )

    def send_weight_grads():
        for c in range(pieces):
            y_copy(c).wait_recv()
            summed = (dw_near[:, c * piece : (c + 1) * piece] + dw_came[c].astype(f32)).astype(bf16)
            dw_own[c] = summed.reshape(n_z, depth, piece)
            copies.start(("z", c), c * n_z + 1, (c + 1) * n_z, z_copy)
        copies.landed.add("y")

    def sum_weight_grads():
        for c in range(pieces):
            copies.arrive(("z", c))
            total = dw_own[c, lane].astype(f32)
            for m in range(c * n_z + 1, (c + 1) * n_z):
                total = total + dw_got[m].astype(f32)
            weight_out[:, c * piece : (c + 1) * piece] = total

    send_weights()
    send_keys()
    send_queries()
    send_upstream()
    regroup()
    send_hidden(0)
    send_hidden(1)
    make_probs()
    make_value_grads()
    send_value_grads()
    project_values(0)
    project_values(1)
    send_partials()
    forward_value_grads()
    copies.settle("s", "k", "p", "q", "u", "b", "w", ("x", 0), ("x", 1), ("e", 0), ("e", 1))
    make_weight_grads()
    sum_values()
    send_weight_grads()
    make_key_grads()
    first_trade()
    copies.settle("a", "f", "r", "y", "dv_swap", "v_swap", "o")
    second_trade()
    end_trade()
    sum_weight_grads()
    copies.finish()


def hand_over(key_ref, weight_ref, key_out, weight_out):
    key_out[...] = key_ref[...]
    weight_out[...] = weight_ref[...]


def on_device(
    hidden, queries, keys, upstream, w_value, segment_ids, response_lengths, advantages, move_plan
):
    n_dp, n_seq = lax.axis_size("dp"), lax.axis_size("seq")
    slots, rows, features = hidden.shape
    length = rows * n_seq
    half = length // 2
    chips = n_seq // 2
    wide = queries.shape[2] * slots // n_seq
    heads = wide // HD
    depth, columns = w_value.shape
    width = depth * n_dp
    share = width // 2
    bf16, f32 = jnp.bfloat16, jnp.float32
    square = (HD // depth) * HD
    tiles = length // TILE
    triangle = TILE * tiles * (tiles + 1) // 2
    dma = pltpu.SemaphoreType.DMA
    key_grads, weight_grads = pl.pallas_call(
        functools.partial(kernel, n_dp, n_seq),
        out_shape=(
            jax.ShapeDtypeStruct((slots, rows, columns), bf16),
            jax.ShapeDtypeStruct((depth, columns), f32),
        ),
        in_specs=[ANY, ANY, ANY, ANY, ANY, ANY, SMEM, VMEM, SMEM],
        out_specs=[VMEM, VMEM],
        scratch_shapes=[
            pltpu.VMEM((slots, rows, features), bf16),
            pltpu.VMEM((square, square), bf16),
            pltpu.VMEM((slots, n_seq, rows, width), bf16),
            pltpu.VMEM((slots, length, width), bf16),
            pltpu.VMEM((2, depth, columns), bf16),
            pltpu.VMEM((2, n_dp // 2, depth, columns), bf16),
            pltpu.VMEM((n_seq, slots, rows), jnp.int32),
            pltpu.VMEM((length, wide), bf16),
            pltpu.VMEM((length, wide), bf16),
            pltpu.VMEM((length, HD), bf16),
            pltpu.VMEM((length, HD), bf16),
            pltpu.VMEM((heads, triangle, TILE), f32),
            pltpu.VMEM((slots, 2, half, columns), bf16),
            pltpu.VMEM((slots, half, columns), bf16),
            pltpu.VMEM((slots, half, columns), bf16),
            pltpu.VMEM((chips, half, HD), bf16),
            pltpu.VMEM((length, HD), f32),
            pltpu.VMEM((half, HD), bf16),
            pltpu.VMEM((half, HD), bf16),
            pltpu.VMEM((n_seq, half, HD), bf16),
            pltpu.VMEM((length, HD), f32),
            pltpu.VMEM((length, HD), bf16),
            pltpu.VMEM((2, slots, rows, columns), bf16),
            pltpu.VMEM((slots, rows, columns), bf16),
            pltpu.VMEM((2, rows, columns), bf16),
            pltpu.VMEM((2, rows, columns), bf16),
            pltpu.VMEM((2, share, columns // 2), bf16),
            pltpu.VMEM((2, share, columns // 2), bf16),
            pltpu.VMEM((share, columns), f32),
            pltpu.VMEM((2, n_dp // 2, depth, columns // 2), bf16),
            pltpu.VMEM((n_dp, depth, columns // 2), bf16),
        ]
        + [dma((n_seq,))] * 10 + [dma((2 * n_seq,))] * 2
        + [dma((n_dp,))] * 2
        + [dma((2,))] * 2
        + [dma((chips,))] * 8
        + [dma((2,))] * 4
        + [dma((n_dp,))] * 2
        + [dma((2,))] * 2
        + [dma((11,))] + [dma((1,))] * 2,
        compiler_params=pltpu.CompilerParams(
            collective_id=0, has_side_effects=True, vmem_limit_bytes=60 << 20
        ),
        name="backward",
    )(
        hidden, queries, keys, upstream, w_value, segment_ids, response_lengths,
        advantages, move_plan.T,
    )
    return pl.pallas_call(
        hand_over,
        out_shape=(
            jax.ShapeDtypeStruct(key_grads.shape, key_grads.dtype),
            jax.ShapeDtypeStruct(weight_grads.shape, weight_grads.dtype),
        ),
        in_specs=[VMEM, VMEM],
        out_specs=[VMEM, VMEM],
        name="hand_over",
    )(key_grads, weight_grads)


def solution(mesh):
    placed = (
        P("dp", "seq", None),
        P("dp", "seq", None),
        P("dp", "seq", None),
        P("dp", "seq", None),
        P(("dp", "seq"), None),
        P("dp", "seq"),
        P("dp", None),
        P("dp", None),
        P(),
    )
    return jax.shard_map(
        on_device,
        mesh=mesh,
        in_specs=placed,
        out_specs=(P("dp", "seq", None), P(("dp", "seq"), None)),
        check_vma=False,
    )
```
